32 devices in a mesh: band: 8 (over z, y), lon: 4 (over x, core).
Axes of the slice: x: 2, y: 2, z: 4, core: 2. Of those that a mesh axis runs over, the one named last changes fastest.
Arguments:
- jacobian: bfloat16 [65536, 137], P(('band', 'lon')), may hold values from -3 to 3
- departure: float32 [65536], P(('band', 'lon')), may hold values from -6 to 6
- inv_var: float32 [65536], P(('band', 'lon')), may hold values from 0.25 to 4
- frac: float32 [2, 65536], P(None, ('band', 'lon')), may hold values from 0 to 1
- anchors: int32 [2, 65536], P(None, ('band', 'lon')), may hold values from 0 to 511, as said below
- counts: int32 [32, 32], P(('band', 'lon')), may hold values from 0 to 64, as said below
Outputs:
- increments: float32 [137, 256, 512], P(None, 'band', 'lon')
The draws below stay inside these ranges and needn't reach their ends.
Inputs may be any that keep to these rules, and one draw needn't show every extreme that they name: counts[p, q] is the number of live slots among the 64 that device p holds for owner q; some pairs reach 64 in every draw, and in every draw some owner receives 64 live slots from every device. `anchors`: every slot that device p holds for owner q has its anchor in owner q's block of 32 latitude rows and 128 longitudes, and its latitude row is at most 254.
All inputs are finite; a program needn't handle non-finite values.
Results may differ from the reference program's by a relative error of at most 0.0041.
Values may be sent and summed in bfloat16 or wider, within the bound.
No kernel may reach another device: no remote copies, remote signals or barrier semaphores. Data moves between devices by JAX's collectives and lax.ppermute only.
A program may use at most 64 MiB of HBM per device.

```python
import math
import jax
import jax.numpy as jnp
from jax import lax

LEV = 137
LAT_DEV = 32
LON_DEV = 128
CAP = 64
SLOTS = 65536
N_BAND = 8
N_LON = 4
DEVICES = 32


def draw_counts(key, part):
    key_width = jax.random.fold_in(key, 11)
    key_jitter = jax.random.fold_in(key, 12)
    key_amount = jax.random.fold_in(key, 13)
    key_owner = jax.random.fold_in(key, 14)
    source_dev = jnp.arange(DEVICES, dtype=jnp.int32)[:, None]
    target_dev = jnp.arange(DEVICES, dtype=jnp.int32)[None, :]
    widths = jax.random.randint(key_width, (DEVICES, 1), max(DEVICES // 8, 1), DEVICES // 2 + 1)
    jitter = jax.random.randint(key_jitter, (DEVICES, 1), 0, max(DEVICES // 16, 1) + 1)
    window_start = (source_dev + jitter) % DEVICES
    inside = (target_dev - window_start) % DEVICES < widths
    amount = jax.random.randint(key_amount, (DEVICES, DEVICES), 1, CAP + 1)
    result = jnp.where(inside, amount, 0)
    result = jnp.where(target_dev == window_start, CAP, result)
    hot_owner = jax.random.randint(key_owner, (), 0, DEVICES)
    result = jnp.where(target_dev == hot_owner, CAP, result)
    return result.astype(jnp.int32)


def draw_anchors(key, part):
    key_lat = jax.random.fold_in(key, 21)
    key_lon = jax.random.fold_in(key, 22)
    total = DEVICES * DEVICES * CAP
    slot_index = jnp.arange(total, dtype=jnp.int32)
    target_dev = slot_index // CAP % DEVICES
    band_of = target_dev // N_LON
    sector_of = target_dev % N_LON
    lat_offset = jax.random.randint(key_lat, (total,), 0, LAT_DEV)
    lat_offset = jnp.where(band_of == N_BAND - 1, jnp.minimum(lat_offset, LAT_DEV - 2), lat_offset)
    lon_offset = jax.random.randint(key_lon, (total,), 0, LON_DEV)
    lat_index = band_of * LAT_DEV + lat_offset
    lon_index = sector_of * LON_DEV + lon_offset
    return jnp.stack([lat_index, lon_index], axis=0).astype(jnp.int32)


def block_scale(rng, dims, shards, smallest, top_value):
    gain, own = 1.0, jax.random.fold_in(rng, 6)
    for dim, shards_of in shards:
        steps = jnp.exp(jax.random.uniform(jax.random.fold_in(own, dim), (shards_of,), jnp.float32, smallest / len(shards), top_value / len(shards)))
        gain = gain * jnp.repeat(steps, dims[dim] // shards_of).reshape([-1 if axis == dim else 1 for axis in range(len(dims))])
    return gain


def gaussian(key, extent, deviation, most, cuts=(), kind=jnp.bfloat16):
    level = block_scale(key, extent, cuts, -0.22, 0.18) if cuts else 1.0
    array = jax.random.normal(key, extent, jnp.float32) * deviation * level
    return jnp.minimum(jnp.maximum(array, -most), most).astype(kind)


def setup_inputs(seed: int = 0) -> dict:
    streams_of = jax.random.split(jax.random.key(seed), 7)
    jacobian = gaussian(streams_of[0], (SLOTS, LEV), 0.5, 3.0, ((0, 32),))
    departure = gaussian(streams_of[1], (SLOTS,), 1.0, 6.0, ((0, 32),), jnp.float32)
    inv_var = jnp.clip(jnp.exp(math.log(4.0) - 2.7725887 * jax.random.uniform(streams_of[2], (SLOTS,), jnp.float32) ** block_scale(streams_of[2], (SLOTS,), ((0, 32),), -0.2, 0.2)), 0.25, 4.0)
    frac = jnp.clip(1.0 * jax.random.uniform(streams_of[3], (2, SLOTS), jnp.float32) ** block_scale(streams_of[3], (2, SLOTS), ((1, 32),), -0.2, 0.2), 0.0, 1.0)
    anchors = draw_anchors(jax.random.fold_in(streams_of[6], 71), 0)
    counts = draw_counts(jax.random.fold_in(streams_of[6], 71), 0)
    return dict(jacobian=jacobian, departure=departure, inv_var=inv_var, frac=frac, anchors=anchors, counts=counts)


def reference(jacobian, departure, inv_var, frac, anchors, counts):
    devices = counts.shape[0]
    row_total = devices * CAP
    nlat = LAT_DEV * N_BAND
    nlon = LON_DEV * N_LON
    within = jnp.arange(CAP, dtype=jnp.int32)

    def one_source(grid_total, source_dev):
        first_row = (source_dev * row_total).astype(jnp.int32)
        jac_rows = lax.dynamic_slice_in_dim(jacobian, first_row, row_total, 0)
        depart_rows = lax.dynamic_slice_in_dim(departure, first_row, row_total, 0)
        inverse_rows = lax.dynamic_slice_in_dim(inv_var, first_row, row_total, 0)
        frac_rows = lax.dynamic_slice_in_dim(frac, first_row, row_total, 1)
        anchor_rows = lax.dynamic_slice_in_dim(anchors, first_row, row_total, 1)
        count_row = lax.dynamic_index_in_dim(counts, source_dev, 0, keepdims=False)
        is_live = (within[None, :] < count_row[:, None]).reshape(row_total)
        forcing = depart_rows * inverse_rows
        adjoint = jnp.where(is_live[:, None], forcing[:, None] * jac_rows.astype(jnp.float32), 0.0).astype(jnp.bfloat16)
        adjoint = lax.optimization_barrier(adjoint).astype(jnp.float32)
        lat_frac = frac_rows[0]
        lon_frac = frac_rows[1]
        corner_exprs = [(1.0 - lat_frac) * (1.0 - lon_frac), (1.0 - lat_frac) * lon_frac,
                        lat_frac * (1.0 - lon_frac), lat_frac * lon_frac]
        lat_index = anchor_rows[0]
        lon_index = anchor_rows[1]
        lon_next = (lon_index + 1) % nlon
        flat_places = [lat_index * nlon + lon_index, lat_index * nlon + lon_next,
                       (lat_index + 1) * nlon + lon_index, (lat_index + 1) * nlon + lon_next]
        for corner in range(4):
            weight = jnp.where(is_live, corner_exprs[corner], 0.0).astype(jnp.bfloat16)
            weight = lax.optimization_barrier(weight).astype(jnp.float32)
            grid_total = grid_total.at[flat_places[corner]].add(adjoint * weight[:, None])
        return grid_total, None

    grid_total = jnp.zeros((nlat * nlon, LEV), jnp.float32)
    grid_total, _ = lax.scan(one_source, grid_total, jnp.arange(devices, dtype=jnp.int32))
    return grid_total.reshape(nlat, nlon, LEV).transpose(2, 0, 1)
```

```python
import functools

import jax
import jax.numpy as jnp
from jax import lax
from jax.experimental import pallas as pl
from jax.experimental.pallas import tpu as pltpu
from jax.sharding import PartitionSpec as P

LAT_DEV = 32
LON_DEV = 128
LANES = 128
N_INFO = 6
F32 = jnp.float32
BF16 = jnp.bfloat16
NT = (((1,), (1,)), ((), ()))
VMEM_LIMIT = 48 * 1024 * 1024


def lane_iota(shape):
    return lax.broadcasted_iota(jnp.int32, shape, len(shape) - 1)


def row_iota(shape):
    return lax.broadcasted_iota(jnp.int32, shape, 0)


def swap_halves(first, second, cap):
    low = lane_iota(first.shape) < cap
    return (
        jnp.where(low, first, pltpu.roll(second, cap, 1)),
        jnp.where(low, pltpu.roll(first, cap, 1), second),
    )


def pack_kernel(counts_ref, jac_ref, dep_ref, inv_ref, frac_ref, anchor_ref, out_ref, *, cap, lon_count):
    levels, slots = jac_ref.shape
    half = out_ref.shape[1]
    body = (levels // 8) * 8
    rest = levels - body
    lane = lane_iota((1, LANES))
    low = lane < cap
    for tile in range(slots // LANES):
        at = pl.ds(tile * LANES, LANES)
        first, second = 2 * tile, 2 * tile + 1
        count = jnp.where(low, counts_ref[0, first], counts_ref[0, second] + cap)
        live = lane < count
        forcing = jnp.where(live, dep_ref[:, at] * inv_ref[:, at], 0.0)
        a = frac_ref[0:1, at]
        b = frac_ref[1:2, at]
        lat0 = jnp.where(low, first // lon_count * LAT_DEV, second // lon_count * LAT_DEV)
        lon0 = jnp.where(low, first % lon_count * LON_DEV, second % lon_count * LON_DEV)
        info = [
            (1.0 - a) * (1.0 - b),
            (1.0 - a) * b,
            a * (1.0 - b),
            a * b,
            (anchor_ref[0:1, at] - lat0).astype(F32),
            (anchor_ref[1:2, at] - lon0).astype(F32),
        ]
        adjoint = jac_ref[0:body, at].astype(F32) * forcing
        tail_rows = 2 * half - body
        tail = jnp.zeros((tail_rows, LANES), F32)
        row = row_iota((tail_rows, LANES))
        for i in range(rest):
            tail = jnp.where(row == i, jac_ref[body + i : body + i + 1, at].astype(F32) * forcing, tail)
        for i, value in enumerate(info):
            tail = jnp.where(row == rest + i, jnp.where(live, value, 0.0), tail)
        whole = jnp.concatenate([adjoint, tail], axis=0)
        one, two = swap_halves(whole[:half], whole[half:], cap)
        out_ref[first] = one.astype(BF16)
        out_ref[second] = two.astype(BF16)


def rim_kernel(recv_ref, x_ref, info_ref, east_ref, north_ref, hot_ref, *, cap, levels):
    devices, half, _ = recv_ref.shape
    body = (levels // 8) * 8
    rest = levels - body
    row = row_iota((LON_DEV, LANES)).astype(F32)
    for tile in range(devices // 2):
        at = pl.ds(tile * LANES, LANES)
        low, high = swap_halves(recv_ref[2 * tile].astype(F32), recv_ref[2 * tile + 1].astype(F32), cap)
        whole = jnp.concatenate([low, high], axis=0)
        x_ref[:, at] = whole.astype(BF16)
        info = whole[body:]
        info_ref[:, at] = info
        w01, w10, w11, lat, lon = [info[rest + i : rest + i + 1] for i in range(1, N_INFO)]
        top = lat == LAT_DEV - 1.0
        w10 = jnp.where(top, w10, 0.0)
        w11_top = jnp.where(top, w11, 0.0)
        hot_ref[0:LON_DEV, at] = jnp.where(
            row == lon, w10, jnp.where(row == lon + 1.0, w11_top, 0.0)
        ).astype(BF16)
        edge = lon == LON_DEV - 1.0
        w01 = jnp.where(edge, w01, 0.0)
        w11 = jnp.where(edge, w11, 0.0)
        hot_ref[LON_DEV:, at] = jnp.where(
            row == lat, w01, jnp.where(row == lat + 1.0, w11, 0.0)
        ).astype(BF16)
    sums = lax.dot_general(x_ref[...], hot_ref[...], NT, preferred_element_type=F32)
    north_ref[...] = sums[:, :LON_DEV]
    east_ref[...] = sums[:, LON_DEV:]


def main_kernel(x_ref, info_ref, out_ref, near_ref, far_ref, lat_ref, *, levels):
    slots = x_ref.shape[1]
    rest = levels % 8
    row = row_iota((LON_DEV, LANES)).astype(F32)
    for tile in range(slots // LANES):
        at = pl.ds(tile * LANES, LANES)
        w00, w01, w10, w11, lat, lon = [info_ref[rest + i : rest + i + 1, at] for i in range(N_INFO)]
        here = row == lon
        after = row == lon + 1.0
        near_ref[:, at] = jnp.where(here, w00, jnp.where(after, w01, 0.0)).astype(BF16)
        far_ref[:, at] = jnp.where(here, w10, jnp.where(after, w11, 0.0)).astype(BF16)
        lat_ref[:, at] = jnp.broadcast_to(lat, (LON_DEV, LANES)).astype(BF16)

    def two_rows(step, carry):
        lat = lat_ref[...]
        near = near_ref[...]
        far = far_ref[...]
        zero = jnp.zeros_like(near)
        hots = []
        for i in range(2):
            r = (2 * step + i).astype(F32).astype(BF16)
            before = (2 * step + i - 1).astype(F32).astype(BF16)
            hots.append(jnp.where(lat == r, near, jnp.where(lat == before, far, zero)))
        hot = jnp.concatenate(hots, axis=0)
        sums = lax.dot_general(x_ref[...], hot, NT, preferred_element_type=F32)
        out_ref[2 * step] = sums[:, :LON_DEV]
        out_ref[2 * step + 1] = sums[:, LON_DEV:]
        return carry

    lax.fori_loop(0, LAT_DEV // 2, two_rows, 0)


def final_kernel(acc_ref, east_ref, north_ref, corner_ref, out_ref):
    rows = acc_ref.shape[1]
    lane = lane_iota((rows, LANES))
    first = lane == 0
    east = east_ref[...]
    for r in range(LAT_DEV):
        value = acc_ref[r] + jnp.where(first, east if r == 0 else pltpu.roll(east, LANES - r, 1), 0.0)
        if r == 0:
            value = value + north_ref[...]
            value = value + jnp.where(first, pltpu.roll(corner_ref[...], LANES - LAT_DEV, 1), 0.0)
        out_ref[pl.ds(r, rows, LAT_DEV), :] = value


def per_device(jacobian, departure, inv_var, frac, anchors, counts, *, n_band, n_lon):
    slots, levels = jacobian.shape
    devices = counts.shape[1]
    cap = slots // devices
    rows = -(-(levels + N_INFO) // 16) * 16
    half = rows // 2
    vmem = pl.BlockSpec(memory_space=pltpu.VMEM)
    smem = pl.BlockSpec(memory_space=pltpu.SMEM)
    params = pltpu.CompilerParams(vmem_limit_bytes=VMEM_LIMIT)
    struct = jax.ShapeDtypeStruct

    payload = pl.pallas_call(
        functools.partial(pack_kernel, cap=cap, lon_count=n_lon),
        out_shape=struct((devices, half, LANES), BF16),
        in_specs=[smem] + [vmem] * 5,
        out_specs=vmem,
        compiler_params=params,
        name="pack",
    )(counts, jacobian.T, departure[None, :], inv_var[None, :], frac, anchors)

    received = lax.all_to_all(payload, ("band", "lon"), split_axis=0, concat_axis=0, tiled=True)

    tail_rows = rows - levels // 8 * 8
    x, info, east, north = pl.pallas_call(
        functools.partial(rim_kernel, cap=cap, levels=levels),
        out_shape=(
            struct((rows, slots), BF16),
            struct((tail_rows, slots), F32),
            struct((rows, LANES), F32),
            struct((rows, LANES), F32),
        ),
        in_specs=[vmem],
        out_specs=(vmem,) * 4,
        scratch_shapes=[pltpu.VMEM((2 * LANES, slots), BF16)],
        compiler_params=params,
        name="rim",
    )(received)

    def place(band, lon):
        return band * n_lon + lon % n_lon

    corner_pairs = [
        (place(i, j), place(i + 1, j + 1)) for i in range(n_band - 1) for j in range(n_lon)
    ]
    corner_in = lax.ppermute(east, ("band", "lon"), corner_pairs)
    east_in = lax.ppermute(east, "lon", [(j, (j + 1) % n_lon) for j in range(n_lon)])
    north_in = lax.ppermute(north, "band", [(i, i + 1) for i in range(n_band - 1)])

    acc = pl.pallas_call(
        functools.partial(main_kernel, levels=levels),
        out_shape=struct((LAT_DEV, rows, LANES), F32),
        in_specs=[vmem] * 2,
        out_specs=vmem,
        scratch_shapes=[pltpu.VMEM((LON_DEV, slots), BF16)] * 3,
        compiler_params=params,
        cost_estimate=pl.CostEstimate(
            flops=2 * rows * slots * LAT_DEV * LON_DEV, bytes_accessed=4 * LAT_DEV * rows * LANES, transcendentals=0
        ),
        name="main",
    )(x, info)

    block = rows // 3
    out = pl.pallas_call(
        final_kernel,
        grid=(3,),
        out_shape=struct((levels * LAT_DEV, LON_DEV), F32),
        in_specs=[pl.BlockSpec((LAT_DEV, block, LANES), lambda i: (0, i, 0))]
        + [pl.BlockSpec((block, LANES), lambda i: (i, 0))] * 3,
        out_specs=pl.BlockSpec((block * LAT_DEV, LON_DEV), lambda i: (i, 0)),
        compiler_params=params,
        name="final",
    )(acc, east_in, north_in, corner_in)
    return out.reshape(levels, LAT_DEV, LON_DEV)


def solution(mesh):
    both = ("band", "lon")
    return jax.shard_map(
        functools.partial(per_device, n_band=mesh.shape["band"], n_lon=mesh.shape["lon"]),
        mesh=mesh,
        in_specs=(P(both, None), P(both), P(both), P(None, both), P(None, both), P(both, None)),
        out_specs=P(None, "band", "lon"),
        check_vma=False,
    )
```

```python
import functools

import jax
import jax.numpy as jnp
from jax import lax
from jax.experimental import pallas as pl
from jax.experimental.pallas import tpu as pltpu
from jax.sharding import PartitionSpec as P

LAT_DEV = 32
LON_DEV = 128
LANES = 128
N_INFO = 6
F32 = jnp.float32
BF16 = jnp.bfloat16
NT = (((1,), (1,)), ((), ()))
VMEM_LIMIT = 48 * 1024 * 1024
VMEM_ALL = 64 * 1024 * 1024
SPAN = 8
STEP_LEVELS = 16
JAC_CHUNKS = 4


def bf(value):
    return jnp.asarray(value, F32).astype(BF16)


def lane_iota(shape):
    return lax.broadcasted_iota(jnp.int32, shape, len(shape) - 1)


def row_iota(shape):
    return lax.broadcasted_iota(jnp.int32, shape, 0)


def swap_halves(first, second, cap):
    low = lane_iota(first.shape) < cap
    return (
        jnp.where(low, first, pltpu.roll(second, cap, 1)),
        jnp.where(low, pltpu.roll(first, cap, 1), second),
    )


def pack_kernel(
    counts_hbm, jac_hbm, dep_hbm, inv_hbm, frac_hbm, anchor_hbm, out_hbm,
    out_ref, counts_ref, jac_ref, dep_ref, inv_ref, frac_ref, anchor_ref, sems, *, cap, lon_count,
):
    levels, slots = jac_ref.shape
    half = out_ref.shape[1]
    body = (levels // 8) * 8
    rest = levels - body
    small = [
        pltpu.make_async_copy(src, dst, sems.at[i])
        for i, (src, dst) in enumerate(
            [
                (counts_hbm, counts_ref),
                (dep_hbm, dep_ref),
                (inv_hbm, inv_ref),
                (frac_hbm, frac_ref),
                (anchor_hbm, anchor_ref),
            ]
        )
    ]
    chunk = slots // JAC_CHUNKS
    large = [
        pltpu.make_async_copy(
            jac_hbm.at[:, pl.ds(i * chunk, chunk)],
            jac_ref.at[:, pl.ds(i * chunk, chunk)],
            sems.at[len(small) + i],
        )
        for i in range(JAC_CHUNKS)
    ]
    for copy in small + large:
        copy.start()
    for copy in small:
        copy.wait()
    stores = []
    lane = lane_iota((1, LANES))
    low = lane < cap
    for tile in range(slots // LANES):
        if tile * LANES % chunk == 0:
            large[tile * LANES // chunk].wait()
        at = pl.ds(tile * LANES, LANES)
        first, second = 2 * tile, 2 * tile + 1
        count = jnp.where(low, counts_ref[0, first], counts_ref[0, second] + cap)
        live = lane < count
        forcing = jnp.where(live, dep_ref[:, at] * inv_ref[:, at], 0.0)
        a = frac_ref[0:1, at]
        b = frac_ref[1:2, at]
        lat0 = jnp.where(low, first // lon_count * LAT_DEV, second // lon_count * LAT_DEV)
        lon0 = jnp.where(low, first % lon_count * LON_DEV, second % lon_count * LON_DEV)
        info = [
            (1.0 - a) * (1.0 - b),
            (1.0 - a) * b,
            a * (1.0 - b),
            a * b,
            (anchor_ref[0:1, at] - lat0).astype(F32),
            (anchor_ref[1:2, at] - lon0).astype(F32),
        ]
        adjoint = jac_ref[0:body, at].astype(F32) * forcing
        tail_rows = 2 * half - body
        tail = jnp.zeros((tail_rows, LANES), F32)
        row = row_iota((tail_rows, LANES))
        for i in range(rest):
            tail = jnp.where(row == i, jac_ref[body + i : body + i + 1, at].astype(F32) * forcing, tail)
        for i, value in enumerate(info):
            tail = jnp.where(row == rest + i, jnp.where(live, value, 0.0), tail)
        whole = jnp.concatenate([adjoint, tail], axis=0)
        one, two = swap_halves(whole[:half], whole[half:], cap)
        out_ref[first] = one.astype(BF16)
        out_ref[second] = two.astype(BF16)
        if (tile + 1) * LANES % chunk == 0:
            done = tile * LANES // chunk
            part = pl.ds(done * chunk // cap, chunk // cap)
            copy = pltpu.make_async_copy(out_ref.at[part], out_hbm.at[part], sems.at[len(small) + JAC_CHUNKS + done])
            copy.start()
            stores.append(copy)
    for copy in stores:
        copy.wait()


def rim_kernel(recv_ref, x_ref, info_ref, east_ref, north_ref, hot_ref, *, cap, levels):
    devices, half, _ = recv_ref.shape
    body = (levels // 8) * 8
    rest = levels - body
    row = row_iota((LON_DEV, LANES)).astype(F32)
    for tile in range(devices // 2):
        at = pl.ds(tile * LANES, LANES)
        low, high = swap_halves(recv_ref[2 * tile].astype(F32), recv_ref[2 * tile + 1].astype(F32), cap)
        whole = jnp.concatenate([low, high], axis=0)
        x_ref[:, at] = whole.astype(BF16)
        info = whole[body:]
        info_ref[:, at] = info
        w01, w10, w11, lat, lon = [info[rest + i : rest + i + 1] for i in range(1, N_INFO)]
        top = lat == LAT_DEV - 1.0
        w10 = jnp.where(top, w10, 0.0)
        w11_top = jnp.where(top, w11, 0.0)
        hot_ref[0:LON_DEV, at] = jnp.where(
            row == lon, w10, jnp.where(row == lon + 1.0, w11_top, 0.0)
        ).astype(BF16)
        edge = lon == LON_DEV - 1.0
        w01 = jnp.where(edge, w01, 0.0)
        w11 = jnp.where(edge, w11, 0.0)
        hot_ref[LON_DEV:, at] = jnp.where(
            row == lat, w01, jnp.where(row == lat + 1.0, w11, 0.0)
        ).astype(BF16)
    sums = lax.dot_general(x_ref[...], hot_ref[...], NT, preferred_element_type=F32)
    north_ref[...] = sums[:, :LON_DEV]
    east_ref[...] = sums[:, LON_DEV:]


def main_kernel(x_ref, info_ref, out_ref, near_ref, far_ref, left_ref, *, levels):
    rows, slots = x_ref.shape
    rest = levels % 8
    row = row_iota((LON_DEV, LANES)).astype(F32)
    for tile in range(slots // LANES):
        at = pl.ds(tile * LANES, LANES)
        w00, w01, w10, w11, _, lon = [info_ref[rest + i : rest + i + 1, at] for i in range(N_INFO)]
        here = row == lon
        after = row == lon + 1.0
        near_ref[:, at] = jnp.where(here, w00, jnp.where(after, w01, 0.0)).astype(BF16)
        far_ref[:, at] = jnp.where(here, w10, jnp.where(after, w11, 0.0)).astype(BF16)
    lat = info_ref[rest + 4 : rest + 5, :]
    group = jnp.floor(lat * (1.0 / SPAN))
    within = (lat - group * SPAN).astype(BF16)
    group = group.astype(BF16)
    lat = lat.astype(BF16)
    groups = LAT_DEV // SPAN
    x = x_ref[...]
    zero_x = jnp.zeros_like(x)
    for u in range(groups):
        left_ref[u * rows : (u + 1) * rows, :] = jnp.where(group == bf(u), x, zero_x)
    zero = jnp.zeros((LON_DEV, slots), BF16)
    far = far_ref[...]
    hot = jnp.concatenate([jnp.where(lat == bf(SPAN * u - 1), far, zero) for u in range(1, groups)], axis=0)
    seam = lax.dot_general(x, hot, NT, preferred_element_type=F32)
    for first in range(0, SPAN, 2):
        hots = []
        for v in (first, first + 1):
            far_part = jnp.where(within == bf(v - 1), far_ref[...], zero) if v else zero
            hots.append(jnp.where(within == bf(v), near_ref[...], far_part))
        sums = lax.dot_general(left_ref[...], jnp.concatenate(hots, axis=0), NT, preferred_element_type=F32)
        for u in range(groups):
            for v in (first, first + 1):
                value = sums[u * rows : (u + 1) * rows, (v - first) * LON_DEV : (v - first + 1) * LON_DEV]
                if v == 0 and u > 0:
                    value = value + seam[:, (u - 1) * LON_DEV : u * LON_DEV]
                out_ref[u * SPAN + v] = value


def final_kernel(acc_ref, east_ref, north_ref, corner_ref, out_hbm, out_ref, sems, *, levels):
    rows = acc_ref.shape[1]
    lane = lane_iota((STEP_LEVELS, LANES))
    first = lane == 0
    copies = []
    for start in range(0, rows, STEP_LEVELS):
        at = pl.ds(start, STEP_LEVELS)
        east = east_ref[at, :]
        for r in range(LAT_DEV):
            value = acc_ref[r, at, :] + jnp.where(first, pltpu.roll(east, LANES - r, 1) if r else east, 0.0)
            if r == 0:
                value = value + north_ref[at, :]
                value = value + jnp.where(first, pltpu.roll(corner_ref[at, :], LANES - LAT_DEV, 1), 0.0)
            out_ref[pl.ds(start * LAT_DEV + r, STEP_LEVELS, LAT_DEV), :] = value
        stop = min(start + STEP_LEVELS, levels)
        span = pl.ds(start * LAT_DEV, (stop - start) * LAT_DEV)
        copy = pltpu.make_async_copy(out_ref.at[span, :], out_hbm.at[span, :], sems.at[len(copies)])
        copy.start()
        copies.append(copy)
    for copy in copies:
        copy.wait()


def per_device(jacobian, departure, inv_var, frac, anchors, counts, *, n_band, n_lon):
    slots, levels = jacobian.shape
    devices = counts.shape[1]
    cap = slots // devices
    rows = -(-(levels + N_INFO) // 16) * 16
    half = rows // 2
    vmem = pl.BlockSpec(memory_space=pltpu.VMEM)
    hbm = pl.BlockSpec(memory_space=pltpu.HBM)
    params = pltpu.CompilerParams(vmem_limit_bytes=VMEM_LIMIT)
    struct = jax.ShapeDtypeStruct

    payload = pl.pallas_call(
        functools.partial(pack_kernel, cap=cap, lon_count=n_lon),
        out_shape=struct((devices, half, LANES), BF16),
        in_specs=[hbm] * 6,
        out_specs=hbm,
        scratch_shapes=[
            pltpu.VMEM((devices, half, LANES), BF16),
            pltpu.SMEM((1, devices), jnp.int32),
            pltpu.VMEM((levels, slots), BF16),
            pltpu.VMEM((1, slots), F32),
            pltpu.VMEM((1, slots), F32),
            pltpu.VMEM((2, slots), F32),
            pltpu.VMEM((2, slots), jnp.int32),
            pltpu.SemaphoreType.DMA((5 + 2 * JAC_CHUNKS,)),
        ],
        compiler_params=pltpu.CompilerParams(vmem_limit_bytes=VMEM_ALL),
        name="pack",
    )(counts, jacobian.T, departure[None, :], inv_var[None, :], frac, anchors)

    received = lax.all_to_all(payload, ("band", "lon"), split_axis=0, concat_axis=0, tiled=True)

    tail_rows = rows - levels // 8 * 8
    x, info, east, north = pl.pallas_call(
        functools.partial(rim_kernel, cap=cap, levels=levels),
        out_shape=(
            struct((rows, slots), BF16),
            struct((tail_rows, slots), F32),
            struct((rows, LANES), F32),
            struct((rows, LANES), F32),
        ),
        in_specs=[vmem],
        out_specs=(vmem,) * 4,
        scratch_shapes=[pltpu.VMEM((2 * LANES, slots), BF16)],
        compiler_params=params,
        name="rim",
    )(received)

    def place(band, lon):
        return band * n_lon + lon % n_lon

    corner_pairs = [
        (place(i, j), place(i + 1, j + 1)) for i in range(n_band - 1) for j in range(n_lon)
    ]
    corner_in = lax.ppermute(east, ("band", "lon"), corner_pairs)
    east_in = lax.ppermute(east, "lon", [(j, (j + 1) % n_lon) for j in range(n_lon)])
    north_in = lax.ppermute(north, "band", [(i, i + 1) for i in range(n_band - 1)])

    acc = pl.pallas_call(
        functools.partial(main_kernel, levels=levels),
        out_shape=struct((LAT_DEV, rows, LANES), F32),
        in_specs=[vmem] * 2,
        out_specs=vmem,
        scratch_shapes=[pltpu.VMEM((LON_DEV, slots), BF16)] * 2
        + [pltpu.VMEM((LAT_DEV // SPAN * rows, slots), BF16)],
        compiler_params=params,
        cost_estimate=pl.CostEstimate(
            flops=2 * rows * slots * LAT_DEV * LON_DEV, bytes_accessed=4 * LAT_DEV * rows * LANES, transcendentals=0
        ),
        name="main",
    )(x, info)

    out = pl.pallas_call(
        functools.partial(final_kernel, levels=levels),
        out_shape=struct((levels * LAT_DEV, LON_DEV), F32),
        in_specs=[vmem] * 4,
        out_specs=hbm,
        scratch_shapes=[
            pltpu.VMEM((rows * LAT_DEV, LON_DEV), F32),
            pltpu.SemaphoreType.DMA((rows // STEP_LEVELS,)),
        ],
        compiler_params=params,
        name="final",
    )(acc, east_in, north_in, corner_in)
    return out.reshape(levels, LAT_DEV, LON_DEV)


def solution(mesh):
    both = ("band", "lon")
    return jax.shard_map(
        functools.partial(per_device, n_band=mesh.shape["band"], n_lon=mesh.shape["lon"]),
        mesh=mesh,
        in_specs=(P(both, None), P(both), P(both), P(None, both), P(None, both), P(both, None)),
        out_specs=P(None, "band", "lon"),
        check_vma=False,
    )
```

```python
import functools

import jax
import jax.numpy as jnp
from jax import lax
from jax.experimental import pallas as pl
from jax.experimental.pallas import tpu as pltpu
from jax.sharding import PartitionSpec as P

LAT_DEV = 32
LON_DEV = 128
LANES = 128
N_INFO = 6
F32 = jnp.float32
BF16 = jnp.bfloat16
NT = (((1,), (1,)), ((), ()))
VMEM_LIMIT = 32 * 1024 * 1024
VMEM_ALL = 64 * 1024 * 1024
SPAN = 8
GROUPS = LAT_DEV // SPAN
LOWER = 4
FOLD = 3
PITCH = LANES // FOLD
JAC_CHUNKS = 4


def bf(value):
    return jnp.asarray(value, F32).astype(BF16)


def lane_iota(shape):
    return lax.broadcasted_iota(jnp.int32, shape, len(shape) - 1)


def row_iota(shape):
    return lax.broadcasted_iota(jnp.int32, shape, 0)


def swap_halves(first, second, cap):
    low = lane_iota(first.shape) < cap
    return (
        jnp.where(low, first, pltpu.roll(second, cap, 1)),
        jnp.where(low, pltpu.roll(first, cap, 1), second),
    )


def pack_kernel(
    counts_hbm, jac_hbm, dep_hbm, inv_hbm, frac_hbm, anchor_hbm, out_hbm,
    out_ref, counts_ref, jac_ref, dep_ref, inv_ref, frac_ref, anchor_ref, sems, *, cap, lon_count,
):
    levels, slots = jac_ref.shape
    half = out_ref.shape[1]
    body = (levels // 8) * 8
    rest = levels - body
    small = [
        pltpu.make_async_copy(src, dst, sems.at[i])
        for i, (src, dst) in enumerate(
            [
                (counts_hbm, counts_ref),
                (dep_hbm, dep_ref),
                (inv_hbm, inv_ref),
                (frac_hbm, frac_ref),
                (anchor_hbm, anchor_ref),
            ]
        )
    ]
    chunk = slots // JAC_CHUNKS
    large = [
        pltpu.make_async_copy(
            jac_hbm.at[:, pl.ds(i * chunk, chunk)],
            jac_ref.at[:, pl.ds(i * chunk, chunk)],
            sems.at[len(small) + i],
        )
        for i in range(JAC_CHUNKS)
    ]
    for copy in small + large:
        copy.start()
    for copy in small:
        copy.wait()
    stores = []
    lane = lane_iota((1, LANES))
    low = lane < cap
    for tile in range(slots // LANES):
        if tile * LANES % chunk == 0:
            large[tile * LANES // chunk].wait()
        at = pl.ds(tile * LANES, LANES)
        first, second = 2 * tile, 2 * tile + 1
        count = jnp.where(low, counts_ref[0, first], counts_ref[0, second] + cap)
        live = lane < count
        forcing = jnp.where(live, dep_ref[:, at] * inv_ref[:, at], 0.0)
        a = frac_ref[0:1, at]
        b = frac_ref[1:2, at]
        lat0 = jnp.where(low, first // lon_count * LAT_DEV, second // lon_count * LAT_DEV)
        lon0 = jnp.where(low, first % lon_count * LON_DEV, second % lon_count * LON_DEV)
        info = [
            (1.0 - a) * (1.0 - b),
            (1.0 - a) * b,
            a * (1.0 - b),
            a * b,
            (anchor_ref[0:1, at] - lat0).astype(F32),
            (anchor_ref[1:2, at] - lon0).astype(F32),
        ]
        adjoint = jac_ref[0:body, at].astype(F32) * forcing
        tail_rows = 2 * half - body
        tail = jnp.zeros((tail_rows, LANES), F32)
        row = row_iota((tail_rows, LANES))
        for i in range(rest):
            tail = jnp.where(row == i, jac_ref[body + i : body + i + 1, at].astype(F32) * forcing, tail)
        for i, value in enumerate(info):
            tail = jnp.where(row == rest + i, jnp.where(live, value, 0.0), tail)
        whole = jnp.concatenate([adjoint, tail], axis=0)
        one, two = swap_halves(whole[:half], whole[half:], cap)
        out_ref[first] = one.astype(BF16)
        out_ref[second] = two.astype(BF16)
        if (tile + 1) * LANES % chunk == 0:
            done = tile * LANES // chunk
            part = pl.ds(done * chunk // cap, chunk // cap)
            copy = pltpu.make_async_copy(out_ref.at[part], out_hbm.at[part], sems.at[len(small) + JAC_CHUNKS + done])
            copy.start()
            stores.append(copy)
    for copy in stores:
        copy.wait()


def rim_kernel(recv_ref, x_ref, info_ref, east_ref, north_ref, hot_ref, *, cap, levels):
    devices, half, _ = recv_ref.shape
    body = (levels // 8) * 8
    rest = levels - body
    row = row_iota((LON_DEV, LANES)).astype(F32)
    for tile in range(devices // 2):
        at = pl.ds(tile * LANES, LANES)
        low, high = swap_halves(recv_ref[2 * tile].astype(F32), recv_ref[2 * tile + 1].astype(F32), cap)
        whole = jnp.concatenate([low, high], axis=0)
        x_ref[:, at] = whole.astype(BF16)
        info = whole[body:]
        info_ref[:, at] = info
        w01, w10, w11, lat, lon = [info[rest + i : rest + i + 1] for i in range(1, N_INFO)]
        top = lat == LAT_DEV - 1.0
        w10 = jnp.where(top, w10, 0.0)
        w11_top = jnp.where(top, w11, 0.0)
        hot_ref[0:LON_DEV, at] = jnp.where(
            row == lon, w10, jnp.where(row == lon + 1.0, w11_top, 0.0)
        ).astype(BF16)
        edge = lon == LON_DEV - 1.0
        w01 = jnp.where(edge, w01, 0.0)
        w11 = jnp.where(edge, w11, 0.0)
        hot_ref[LON_DEV:, at] = jnp.where(
            row == lat, w01, jnp.where(row == lat + 1.0, w11, 0.0)
        ).astype(BF16)
    sums = lax.dot_general(x_ref[...], hot_ref[...], NT, preferred_element_type=F32)
    north_ref[...] = sums[:, :LON_DEV]
    block = east_ref.shape[0]
    east = sums[:block, LON_DEV:]
    for g in range(1, FOLD):
        east = east + pltpu.roll(sums[g * block : (g + 1) * block, LON_DEV:], g * PITCH, 1)
    east_ref[...] = east


def hot_rows(near_ref, far_ref, within, first, count):
    zero = jnp.zeros(near_ref.shape, BF16)
    hots = []
    for v in range(first, first + count):
        far_part = jnp.where(within == bf(v - 1), far_ref[...], zero) if v else zero
        hots.append(jnp.where(within == bf(v), near_ref[...], far_part))
    return jnp.concatenate(hots, axis=0)


def split_latitude(lat):
    group = jnp.floor(lat * (1.0 / SPAN))
    return group.astype(BF16), (lat - group * SPAN).astype(BF16)


def lower_kernel(x_ref, info_ref, acc_ref, near_ref, far_ref, left_ref, *, levels):
    rows, slots = x_ref.shape
    rest = levels % 8
    row = row_iota((LON_DEV, LANES)).astype(F32)
    for tile in range(slots // LANES):
        at = pl.ds(tile * LANES, LANES)
        w00, w01, w10, w11, _, lon = [info_ref[rest + i : rest + i + 1, at] for i in range(N_INFO)]
        here = row == lon
        after = row == lon + 1.0
        near_ref[:, at] = jnp.where(here, w00, jnp.where(after, w01, 0.0)).astype(BF16)
        far_ref[:, at] = jnp.where(here, w10, jnp.where(after, w11, 0.0)).astype(BF16)
    lat = info_ref[rest + 4 : rest + 5, :]
    group, within = split_latitude(lat)
    lat = lat.astype(BF16)
    x = x_ref[...]
    zero_x = jnp.zeros_like(x)
    for u in range(GROUPS):
        left_ref[u * rows : (u + 1) * rows, :] = jnp.where(group == bf(u), x, zero_x)
    zero = jnp.zeros((LON_DEV, slots), BF16)
    far = far_ref[...]
    hot = jnp.concatenate([jnp.where(lat == bf(SPAN * u - 1), far, zero) for u in range(1, GROUPS)], axis=0)
    seam = lax.dot_general(x, hot, NT, preferred_element_type=F32)
    for first in range(0, LOWER, 2):
        hot = hot_rows(near_ref, far_ref, within, first, 2)
        sums = lax.dot_general(left_ref[...], hot, NT, preferred_element_type=F32)
        for u in range(GROUPS):
            for i in range(2):
                value = sums[u * rows : (u + 1) * rows, i * LON_DEV : (i + 1) * LON_DEV]
                if first + i == 0 and u > 0:
                    value = value + seam[:, (u - 1) * LON_DEV : u * LON_DEV]
                acc_ref[u * LOWER + first + i] = value


def edge_column(fold, r, first_lane):
    parts = []
    for g in range(FOLD):
        shift = (LANES - g * PITCH - r) % LANES
        parts.append(pltpu.roll(fold, shift, 1) if shift else fold)
    return jnp.where(first_lane, jnp.concatenate(parts, axis=0), 0.0)


def upper_kernel(
    acc_ref, near_ref, far_ref, left_ref, info_ref, east_ref, out_hbm, south_ref, grid_ref, sems, *, levels
):
    rows = acc_ref.shape[1]
    rest = levels % 8
    first_lane = lane_iota((rows, LANES)) == 0
    copies = []

    def finish(r, value):
        value = value + edge_column(east_ref[...], r, first_lane)
        if r == 0:
            south_ref[...] = value
            return
        grid_ref[r] = value
        copy = pltpu.make_async_copy(grid_ref.at[r, 0:levels, :], out_hbm.at[:, r, :], sems.at[r])
        copy.start()
        copies.append(copy)

    for u in range(GROUPS):
        for v in range(LOWER):
            finish(u * SPAN + v, acc_ref[u * LOWER + v])
    _, within = split_latitude(info_ref[rest + 4 : rest + 5, :])
    for first in range(LOWER, SPAN, 2):
        hot = hot_rows(near_ref, far_ref, within, first, 2)
        sums = lax.dot_general(left_ref[...], hot, NT, preferred_element_type=F32)
        for u in range(GROUPS):
            for i in range(2):
                finish(
                    u * SPAN + first + i,
                    sums[u * rows : (u + 1) * rows, i * LON_DEV : (i + 1) * LON_DEV],
                )
    for copy in copies:
        copy.wait()


def last_kernel(south_ref, north_ref, corner_ref, grid_hbm, out_hbm, row_ref, sem):
    del grid_hbm
    first_lane = lane_iota(south_ref.shape) == 0
    passed = north_ref[...] + edge_column(corner_ref[...], LAT_DEV, first_lane)
    row_ref[...] = south_ref[...] + jnp.where(lax.axis_index("band") > 0, passed, 0.0)
    copy = pltpu.make_async_copy(row_ref.at[0 : out_hbm.shape[0], :], out_hbm.at[:, 0, :], sem)
    copy.start()
    copy.wait()


def per_device(jacobian, departure, inv_var, frac, anchors, counts, *, n_band, n_lon):
    slots, levels = jacobian.shape
    devices = counts.shape[1]
    cap = slots // devices
    rows = -(-(levels + N_INFO) // 16) * 16
    half = rows // 2
    vmem = pl.BlockSpec(memory_space=pltpu.VMEM)
    hbm = pl.BlockSpec(memory_space=pltpu.HBM)
    params = pltpu.CompilerParams(vmem_limit_bytes=VMEM_LIMIT)
    struct = jax.ShapeDtypeStruct

    payload = pl.pallas_call(
        functools.partial(pack_kernel, cap=cap, lon_count=n_lon),
        out_shape=struct((devices, half, LANES), BF16),
        in_specs=[hbm] * 6,
        out_specs=hbm,
        scratch_shapes=[
            pltpu.VMEM((devices, half, LANES), BF16),
            pltpu.SMEM((1, devices), jnp.int32),
            pltpu.VMEM((levels, slots), BF16),
            pltpu.VMEM((1, slots), F32),
            pltpu.VMEM((1, slots), F32),
            pltpu.VMEM((2, slots), F32),
            pltpu.VMEM((2, slots), jnp.int32),
            pltpu.SemaphoreType.DMA((5 + 2 * JAC_CHUNKS,)),
        ],
        compiler_params=pltpu.CompilerParams(vmem_limit_bytes=VMEM_ALL),
        name="pack",
    )(counts, jacobian.T, departure[None, :], inv_var[None, :], frac, anchors)

    received = lax.all_to_all(payload, ("band", "lon"), split_axis=0, concat_axis=0, tiled=True)

    tail_rows = rows - levels // 8 * 8
    x, info, east, north = pl.pallas_call(
        functools.partial(rim_kernel, cap=cap, levels=levels),
        out_shape=(
            struct((rows, slots), BF16),
            struct((tail_rows, slots), F32),
            struct((rows // FOLD, LANES), F32),
            struct((rows, LANES), F32),
        ),
        in_specs=[vmem],
        out_specs=(vmem,) * 4,
        scratch_shapes=[pltpu.VMEM((2 * LANES, slots), BF16)],
        compiler_params=params,
        name="rim",
    )(received)

    bands, lons = range(n_band), range(n_lon)
    north_in = lax.ppermute(north, "band", [(i, (i + 1) % n_band) for i in bands])
    corner_in = lax.ppermute(
        east,
        ("band", "lon"),
        [(i * n_lon + j, (i + 1) % n_band * n_lon + (j + 1) % n_lon) for i in bands for j in lons],
    )
    east_in = lax.ppermute(east, "lon", [(j, (j + 1) % n_lon) for j in lons])

    acc, near, far, left = pl.pallas_call(
        functools.partial(lower_kernel, levels=levels),
        out_shape=(
            struct((GROUPS * LOWER, rows, LANES), F32),
            struct((LON_DEV, slots), BF16),
            struct((LON_DEV, slots), BF16),
            struct((GROUPS * rows, slots), BF16),
        ),
        in_specs=[vmem] * 2,
        out_specs=(vmem,) * 4,
        compiler_params=params,
        name="lower",
    )(x, info)

    grid, south = pl.pallas_call(
        functools.partial(upper_kernel, levels=levels),
        out_shape=(struct((levels, LAT_DEV, LON_DEV), F32), struct((rows, LANES), F32)),
        in_specs=[vmem] * 6,
        out_specs=(hbm, vmem),
        scratch_shapes=[pltpu.VMEM((LAT_DEV, rows, LANES), F32), pltpu.SemaphoreType.DMA((LAT_DEV,))],
        compiler_params=params,
        name="upper",
    )(acc, near, far, left, info, east_in)

    return pl.pallas_call(
        last_kernel,
        out_shape=struct((levels, LAT_DEV, LON_DEV), F32),
        in_specs=[vmem, vmem, vmem, hbm],
        out_specs=hbm,
        scratch_shapes=[pltpu.VMEM((rows, LANES), F32), pltpu.SemaphoreType.DMA],
        input_output_aliases={3: 0},
        compiler_params=params,
        name="last",
    )(south, north_in, corner_in, grid)


def solution(mesh):
    both = ("band", "lon")
    return jax.shard_map(
        functools.partial(per_device, n_band=mesh.shape["band"], n_lon=mesh.shape["lon"]),
        mesh=mesh,
        in_specs=(P(both, None), P(both), P(both), P(None, both), P(None, both), P(both, None)),
        out_specs=P(None, "band", "lon"),
        check_vma=False,
    )
```

```python
import functools

import jax
import jax.numpy as jnp
from jax import lax
from jax.experimental import pallas as pl
from jax.experimental.pallas import tpu as pltpu
from jax.sharding import PartitionSpec as P

LAT_DEV = 32
LON_DEV = 128
LANES = 128
N_INFO = 6
F32 = jnp.float32
BF16 = jnp.bfloat16
NT = (((1,), (1,)), ((), ()))
VMEM_LIMIT = 32 * 1024 * 1024
VMEM_ALL = 64 * 1024 * 1024
SPAN = 8
GROUPS = LAT_DEV // SPAN
LOWER = 6
EDGE_ROWS = -(-(LAT_DEV + 1) // 16) * 16
FOLD = 3
PITCH = LANES // FOLD
JAC_CHUNKS = 2


def bf(value):
    return jnp.asarray(value, F32).astype(BF16)


def lane_iota(shape):
    return lax.broadcasted_iota(jnp.int32, shape, len(shape) - 1)


def row_iota(shape):
    return lax.broadcasted_iota(jnp.int32, shape, 0)


def swap_halves(first, second, cap):
    low = lane_iota(first.shape) < cap
    return (
        jnp.where(low, first, pltpu.roll(second, cap, 1)),
        jnp.where(low, pltpu.roll(first, cap, 1), second),
    )


def pack_kernel(
    counts_hbm, jac_hbm, dep_hbm, inv_hbm, frac_hbm, anchor_hbm, out_hbm,
    out_ref, counts_ref, jac_ref, dep_ref, inv_ref, frac_ref, anchor_ref, sems, *, cap, lon_count,
):
    levels, slots = jac_ref.shape
    half = out_ref.shape[1]
    body = (levels // 8) * 8
    rest = levels - body
    small = [
        pltpu.make_async_copy(src, dst, sems.at[i])
        for i, (src, dst) in enumerate(
            [
                (counts_hbm, counts_ref),
                (dep_hbm, dep_ref),
                (inv_hbm, inv_ref),
                (frac_hbm, frac_ref),
                (anchor_hbm, anchor_ref),
            ]
        )
    ]
    chunk = slots // JAC_CHUNKS
    large = [
        pltpu.make_async_copy(
            jac_hbm.at[:, pl.ds(i * chunk, chunk)],
            jac_ref.at[:, pl.ds(i * chunk, chunk)],
            sems.at[len(small) + i],
        )
        for i in range(JAC_CHUNKS)
    ]
    for copy in small + large:
        copy.start()
    for copy in small:
        copy.wait()
    stores = []
    lane = lane_iota((1, LANES))
    low = lane < cap
    for tile in range(slots // LANES):
        if tile * LANES % chunk == 0:
            large[tile * LANES // chunk].wait()
        at = pl.ds(tile * LANES, LANES)
        first, second = 2 * tile, 2 * tile + 1
        count = jnp.where(low, counts_ref[0, first], counts_ref[0, second] + cap)
        live = lane < count
        forcing = jnp.where(live, dep_ref[:, at] * inv_ref[:, at], 0.0)
        a = frac_ref[0:1, at]
        b = frac_ref[1:2, at]
        lat0 = jnp.where(low, first // lon_count * LAT_DEV, second // lon_count * LAT_DEV)
        lon0 = jnp.where(low, first % lon_count * LON_DEV, second % lon_count * LON_DEV)
        info = [
            (1.0 - a) * (1.0 - b),
            (1.0 - a) * b,
            a * (1.0 - b),
            a * b,
            (anchor_ref[0:1, at] - lat0).astype(F32),
            (anchor_ref[1:2, at] - lon0).astype(F32),
        ]
        adjoint = jac_ref[0:body, at].astype(F32) * forcing
        tail_rows = 2 * half - body
        tail = jnp.zeros((tail_rows, LANES), F32)
        row = row_iota((tail_rows, LANES))
        for i in range(rest):
            tail = jnp.where(row == i, jac_ref[body + i : body + i + 1, at].astype(F32) * forcing, tail)
        for i, value in enumerate(info):
            tail = jnp.where(row == rest + i, jnp.where(live, value, 0.0), tail)
        whole = jnp.concatenate([adjoint, tail], axis=0)
        one, two = swap_halves(whole[:half], whole[half:], cap)
        out_ref[first] = one.astype(BF16)
        out_ref[second] = two.astype(BF16)
        if (tile + 1) * LANES % chunk == 0:
            done = tile * LANES // chunk
            part = pl.ds(done * chunk // cap, chunk // cap)
            copy = pltpu.make_async_copy(out_ref.at[part], out_hbm.at[part], sems.at[len(small) + JAC_CHUNKS + done])
            copy.start()
            stores.append(copy)
    for copy in stores:
        copy.wait()


def rim_kernel(recv_ref, x_ref, info_ref, east_ref, north_ref, corner_ref, hot_ref, *, cap, levels):
    devices, half, _ = recv_ref.shape
    body = (levels // 8) * 8
    rest = levels - body
    row = row_iota((LON_DEV, LANES)).astype(F32)
    for tile in range(devices // 2):
        at = pl.ds(tile * LANES, LANES)
        low, high = swap_halves(recv_ref[2 * tile].astype(F32), recv_ref[2 * tile + 1].astype(F32), cap)
        whole = jnp.concatenate([low, high], axis=0)
        x_ref[:, at] = whole.astype(BF16)
        info = whole[body:]
        info_ref[:, at] = info
        w01, w10, w11, lat, lon = [info[rest + i : rest + i + 1] for i in range(1, N_INFO)]
        top = lat == LAT_DEV - 1.0
        w10 = jnp.where(top, w10, 0.0)
        w11_top = jnp.where(top, w11, 0.0)
        hot_ref[0:LON_DEV, at] = jnp.where(
            row == lon, w10, jnp.where(row == lon + 1.0, w11_top, 0.0)
        ).astype(BF16)
        edge = lon == LON_DEV - 1.0
        w01 = jnp.where(edge, w01, 0.0)
        w11 = jnp.where(edge, w11, 0.0)
        few = row[:EDGE_ROWS]
        hot_ref[LON_DEV : LON_DEV + EDGE_ROWS, at] = jnp.where(
            few == lat, w01, jnp.where(few == lat + 1.0, w11, 0.0)
        ).astype(BF16)
    hot_ref[LON_DEV + EDGE_ROWS :, :] = jnp.zeros((LANES - EDGE_ROWS, x_ref.shape[1]), BF16)
    sums = lax.dot_general(x_ref[...], hot_ref[...], NT, preferred_element_type=F32)
    north_ref[...] = sums[:, :LON_DEV].astype(BF16)
    block = east_ref.shape[0]
    east = sums[:block, LON_DEV:]
    for g in range(1, FOLD):
        east = east + pltpu.roll(sums[g * block : (g + 1) * block, LON_DEV:], g * PITCH, 1)
    east_ref[...] = east
    corner_ref[:block] = east
    corner_ref[block:] = east


def hot_rows(near_ref, far_ref, within, first, count):
    zero = jnp.zeros(near_ref.shape, BF16)
    hots = []
    for v in range(first, first + count):
        far_part = jnp.where(within == bf(v - 1), far_ref[...], zero) if v else zero
        hots.append(jnp.where(within == bf(v), near_ref[...], far_part))
    return jnp.concatenate(hots, axis=0)


def split_latitude(lat):
    group = jnp.floor(lat * (1.0 / SPAN))
    return group.astype(BF16), (lat - group * SPAN).astype(BF16)


def lower_kernel(x_ref, info_ref, acc_ref, near_ref, far_ref, left_ref, *, levels):
    rows, slots = x_ref.shape
    rest = levels % 8
    row = row_iota((LON_DEV, LANES)).astype(F32)
    for tile in range(slots // LANES):
        at = pl.ds(tile * LANES, LANES)
        w00, w01, w10, w11, _, lon = [info_ref[rest + i : rest + i + 1, at] for i in range(N_INFO)]
        here = row == lon
        after = row == lon + 1.0
        near_ref[:, at] = jnp.where(here, w00, jnp.where(after, w01, 0.0)).astype(BF16)
        far_ref[:, at] = jnp.where(here, w10, jnp.where(after, w11, 0.0)).astype(BF16)
    lat = info_ref[rest + 4 : rest + 5, :]
    group, within = split_latitude(lat)
    lat = lat.astype(BF16)
    x = x_ref[...]
    zero_x = jnp.zeros_like(x)
    for u in range(GROUPS):
        left_ref[u * rows : (u + 1) * rows, :] = jnp.where(group == bf(u), x, zero_x)
    zero = jnp.zeros((LON_DEV, slots), BF16)
    far = far_ref[...]
    hot = jnp.concatenate([jnp.where(lat == bf(SPAN * u - 1), far, zero) for u in range(1, GROUPS)], axis=0)
    seam = lax.dot_general(x, hot, NT, preferred_element_type=F32)
    for first in range(0, LOWER, 2):
        hot = hot_rows(near_ref, far_ref, within, first, 2)
        sums = lax.dot_general(left_ref[...], hot, NT, preferred_element_type=F32)
        for u in range(GROUPS):
            for i in range(2):
                value = sums[u * rows : (u + 1) * rows, i * LON_DEV : (i + 1) * LON_DEV]
                if first + i == 0 and u > 0:
                    value = value + seam[:, (u - 1) * LON_DEV : u * LON_DEV]
                acc_ref[u * LOWER + first + i] = value


def edge_column(fold, r, first_lane):
    parts = []
    for g in range(FOLD):
        shift = (LANES - g * PITCH - r) % LANES
        parts.append(pltpu.roll(fold, shift, 1) if shift else fold)
    return jnp.where(first_lane, jnp.concatenate(parts, axis=0), 0.0)


def upper_kernel(
    acc_ref, near_ref, far_ref, left_ref, info_ref, east_ref, out_hbm, south_ref, grid_ref, sems, *, levels
):
    rows = acc_ref.shape[1]
    rest = levels % 8
    first_lane = lane_iota((rows, LANES)) == 0
    copies = []

    def finish(r, value):
        value = value + edge_column(east_ref[...], r, first_lane)
        if r == 0:
            south_ref[...] = value
            return
        grid_ref[r] = value
        copy = pltpu.make_async_copy(grid_ref.at[r, 0:levels, :], out_hbm.at[:, r, :], sems.at[r])
        copy.start()
        copies.append(copy)

    for u in range(GROUPS):
        for v in range(LOWER):
            finish(u * SPAN + v, acc_ref[u * LOWER + v])
    _, within = split_latitude(info_ref[rest + 4 : rest + 5, :])
    for first in range(LOWER, SPAN, 2):
        hot = hot_rows(near_ref, far_ref, within, first, 2)
        sums = lax.dot_general(left_ref[...], hot, NT, preferred_element_type=F32)
        for u in range(GROUPS):
            for i in range(2):
                finish(
                    u * SPAN + first + i,
                    sums[u * rows : (u + 1) * rows, i * LON_DEV : (i + 1) * LON_DEV],
                )
    for copy in copies:
        copy.wait()


def last_kernel(south_ref, north_ref, corner_ref, grid_hbm, out_hbm, row_ref, sem):
    del grid_hbm
    first_lane = lane_iota(south_ref.shape) == 0
    passed = north_ref[...].astype(F32) + edge_column(corner_ref[: corner_ref.shape[0] // 2], LAT_DEV, first_lane)
    row_ref[...] = south_ref[...] + jnp.where(lax.axis_index("band") > 0, passed, 0.0)
    copy = pltpu.make_async_copy(row_ref.at[0 : out_hbm.shape[0], :], out_hbm.at[:, 0, :], sem)
    copy.start()
    copy.wait()


def per_device(jacobian, departure, inv_var, frac, anchors, counts, *, n_band, n_lon):
    slots, levels = jacobian.shape
    devices = counts.shape[1]
    cap = slots // devices
    rows = -(-(levels + N_INFO) // 16) * 16
    half = rows // 2
    vmem = pl.BlockSpec(memory_space=pltpu.VMEM)
    hbm = pl.BlockSpec(memory_space=pltpu.HBM)
    params = pltpu.CompilerParams(vmem_limit_bytes=VMEM_LIMIT)
    struct = jax.ShapeDtypeStruct

    payload = pl.pallas_call(
        functools.partial(pack_kernel, cap=cap, lon_count=n_lon),
        out_shape=struct((devices, half, LANES), BF16),
        in_specs=[hbm] * 6,
        out_specs=hbm,
        scratch_shapes=[
            pltpu.VMEM((devices, half, LANES), BF16),
            pltpu.SMEM((1, devices), jnp.int32),
            pltpu.VMEM((levels, slots), BF16),
            pltpu.VMEM((1, slots), F32),
            pltpu.VMEM((1, slots), F32),
            pltpu.VMEM((2, slots), F32),
            pltpu.VMEM((2, slots), jnp.int32),
            pltpu.SemaphoreType.DMA((5 + 2 * JAC_CHUNKS,)),
        ],
        compiler_params=pltpu.CompilerParams(vmem_limit_bytes=VMEM_ALL),
        name="pack",
    )(counts, jacobian.T, departure[None, :], inv_var[None, :], frac, anchors)

    received = lax.all_to_all(payload, ("band", "lon"), split_axis=0, concat_axis=0, tiled=True)

    tail_rows = rows - levels // 8 * 8
    x, info, east, north, corner = pl.pallas_call(
        functools.partial(rim_kernel, cap=cap, levels=levels),
        out_shape=(
            struct((rows, slots), BF16),
            struct((tail_rows, slots), F32),
            struct((rows // FOLD, LANES), F32),
            struct((rows, LANES), BF16),
            struct((rows // FOLD * 2, LANES), F32),
        ),
        in_specs=[vmem],
        out_specs=(vmem,) * 5,
        scratch_shapes=[pltpu.VMEM((2 * LANES, slots), BF16)],
        compiler_params=params,
        name="rim",
    )(received)

    bands, lons = range(n_band), range(n_lon)
    north_in = lax.ppermute(north, "band", [(i, (i + 1) % n_band) for i in bands])
    corner_in = lax.ppermute(
        corner,
        ("band", "lon"),
        [(i * n_lon + j, (i + 1) % n_band * n_lon + (j + 1) % n_lon) for i in bands for j in lons],
    )
    east_in = lax.ppermute(east, "lon", [(j, (j + 1) % n_lon) for j in lons])

    acc, near, far, left = pl.pallas_call(
        functools.partial(lower_kernel, levels=levels),
        out_shape=(
            struct((GROUPS * LOWER, rows, LANES), F32),
            struct((LON_DEV, slots), BF16),
            struct((LON_DEV, slots), BF16),
            struct((GROUPS * rows, slots), BF16),
        ),
        in_specs=[vmem] * 2,
        out_specs=(vmem,) * 4,
        compiler_params=params,
        name="lower",
    )(x, info)

    grid, south = pl.pallas_call(
        functools.partial(upper_kernel, levels=levels),
        out_shape=(struct((levels, LAT_DEV, LON_DEV), F32), struct((rows, LANES), F32)),
        in_specs=[vmem] * 6,
        out_specs=(hbm, vmem),
        scratch_shapes=[pltpu.VMEM((LAT_DEV, rows, LANES), F32), pltpu.SemaphoreType.DMA((LAT_DEV,))],
        compiler_params=params,
        name="upper",
    )(acc, near, far, left, info, east_in)

    return pl.pallas_call(
        last_kernel,
        out_shape=struct((levels, LAT_DEV, LON_DEV), F32),
        in_specs=[vmem, vmem, vmem, hbm],
        out_specs=hbm,
        scratch_shapes=[pltpu.VMEM((rows, LANES), F32), pltpu.SemaphoreType.DMA],
        input_output_aliases={3: 0},
        compiler_params=params,
        name="last",
    )(south, north_in, corner_in, grid)


def solution(mesh):
    both = ("band", "lon")
    return jax.shard_map(
        functools.partial(per_device, n_band=mesh.shape["band"], n_lon=mesh.shape["lon"]),
        mesh=mesh,
        in_specs=(P(both, None), P(both), P(both), P(None, both), P(None, both), P(both, None)),
        out_specs=P(None, "band", "lon"),
        check_vma=False,
    )
```

```python
import functools

import jax
import jax.numpy as jnp
from jax import lax
from jax.experimental import pallas as pl
from jax.experimental.pallas import tpu as pltpu
from jax.sharding import PartitionSpec as P

LAT_DEV = 32
LON_DEV = 128
LANES = 128
N_INFO = 6
F32 = jnp.float32
BF16 = jnp.bfloat16
NT = (((1,), (1,)), ((), ()))
VMEM_LIMIT = 32 * 1024 * 1024
VMEM_ALL = 64 * 1024 * 1024
SPAN = 16
GROUPS = LAT_DEV // SPAN
LOWER = 12
EDGE_ROWS = -(-(LAT_DEV + 1) // 16) * 16
FOLD = 3
PITCH = LANES // FOLD
JAC_CHUNKS = 2


def bf(value):
    return jnp.asarray(value, F32).astype(BF16)


def lane_iota(shape):
    return lax.broadcasted_iota(jnp.int32, shape, len(shape) - 1)


def row_iota(shape):
    return lax.broadcasted_iota(jnp.int32, shape, 0)


def swap_halves(first, second, cap):
    low = lane_iota(first.shape) < cap
    return (
        jnp.where(low, first, pltpu.roll(second, cap, 1)),
        jnp.where(low, pltpu.roll(first, cap, 1), second),
    )


def pack_kernel(
    counts_hbm, jac_hbm, dep_hbm, inv_hbm, frac_hbm, anchor_hbm, out_hbm,
    out_ref, counts_ref, jac_ref, dep_ref, inv_ref, frac_ref, anchor_ref, sems, *, cap, lon_count,
):
    levels, slots = jac_ref.shape
    half = out_ref.shape[1]
    body = (levels // 8) * 8
    rest = levels - body
    small = [
        pltpu.make_async_copy(src, dst, sems.at[i])
        for i, (src, dst) in enumerate(
            [
                (counts_hbm, counts_ref),
                (dep_hbm, dep_ref),
                (inv_hbm, inv_ref),
                (frac_hbm, frac_ref),
                (anchor_hbm, anchor_ref),
            ]
        )
    ]
    chunk = slots // JAC_CHUNKS
    large = [
        pltpu.make_async_copy(
            jac_hbm.at[:, pl.ds(i * chunk, chunk)],
            jac_ref.at[:, pl.ds(i * chunk, chunk)],
            sems.at[len(small) + i],
        )
        for i in range(JAC_CHUNKS)
    ]
    for copy in small + large:
        copy.start()
    for copy in small:
        copy.wait()
    stores = []
    lane = lane_iota((1, LANES))
    low = lane < cap
    for tile in range(slots // LANES):
        if tile * LANES % chunk == 0:
            large[tile * LANES // chunk].wait()
        at = pl.ds(tile * LANES, LANES)
        first, second = 2 * tile, 2 * tile + 1
        count = jnp.where(low, counts_ref[0, first], counts_ref[0, second] + cap)
        live = lane < count
        forcing = jnp.where(live, dep_ref[:, at] * inv_ref[:, at], 0.0)
        a = frac_ref[0:1, at]
        b = frac_ref[1:2, at]
        lat0 = jnp.where(low, first // lon_count * LAT_DEV, second // lon_count * LAT_DEV)
        lon0 = jnp.where(low, first % lon_count * LON_DEV, second % lon_count * LON_DEV)
        info = [
            (1.0 - a) * (1.0 - b),
            (1.0 - a) * b,
            a * (1.0 - b),
            a * b,
            (anchor_ref[0:1, at] - lat0).astype(F32),
            (anchor_ref[1:2, at] - lon0).astype(F32),
        ]
        adjoint = jac_ref[0:body, at].astype(F32) * forcing
        tail_rows = 2 * half - body
        tail = jnp.zeros((tail_rows, LANES), F32)
        row = row_iota((tail_rows, LANES))
        for i in range(rest):
            tail = jnp.where(row == i, jac_ref[body + i : body + i + 1, at].astype(F32) * forcing, tail)
        for i, value in enumerate(info):
            tail = jnp.where(row == rest + i, jnp.where(live, value, 0.0), tail)
        whole = jnp.concatenate([adjoint, tail], axis=0)
        one, two = swap_halves(whole[:half], whole[half:], cap)
        out_ref[first] = one.astype(BF16)
        out_ref[second] = two.astype(BF16)
        if (tile + 1) * LANES % chunk == 0:
            done = tile * LANES // chunk
            part = pl.ds(done * chunk // cap, chunk // cap)
            copy = pltpu.make_async_copy(out_ref.at[part], out_hbm.at[part], sems.at[len(small) + JAC_CHUNKS + done])
            copy.start()
            stores.append(copy)
    for copy in stores:
        copy.wait()


def rim_kernel(recv_ref, x_ref, info_ref, east_ref, north_ref, corner_ref, hot_ref, *, cap, levels):
    devices, half, _ = recv_ref.shape
    body = (levels // 8) * 8
    rest = levels - body
    row = row_iota((LON_DEV, LANES)).astype(F32)
    for tile in range(devices // 2):
        at = pl.ds(tile * LANES, LANES)
        low, high = swap_halves(recv_ref[2 * tile].astype(F32), recv_ref[2 * tile + 1].astype(F32), cap)
        whole = jnp.concatenate([low, high], axis=0)
        x_ref[:, at] = whole.astype(BF16)
        info = whole[body:]
        info_ref[:, at] = info
        w01, w10, w11, lat, lon = [info[rest + i : rest + i + 1] for i in range(1, N_INFO)]
        top = lat == LAT_DEV - 1.0
        w10 = jnp.where(top, w10, 0.0)
        w11_top = jnp.where(top, w11, 0.0)
        hot_ref[0:LON_DEV, at] = jnp.where(
            row == lon, w10, jnp.where(row == lon + 1.0, w11_top, 0.0)
        ).astype(BF16)
        edge = lon == LON_DEV - 1.0
        w01 = jnp.where(edge, w01, 0.0)
        w11 = jnp.where(edge, w11, 0.0)
        few = row[:EDGE_ROWS]
        hot_ref[LON_DEV : LON_DEV + EDGE_ROWS, at] = jnp.where(
            few == lat, w01, jnp.where(few == lat + 1.0, w11, 0.0)
        ).astype(BF16)
    hot_ref[LON_DEV + EDGE_ROWS :, :] = jnp.zeros((LANES - EDGE_ROWS, x_ref.shape[1]), BF16)
    sums = lax.dot_general(x_ref[...], hot_ref[...], NT, preferred_element_type=F32)
    north_ref[...] = sums[:, :LON_DEV].astype(BF16)
    block = east_ref.shape[0]
    east = sums[:block, LON_DEV:]
    for g in range(1, FOLD):
        east = east + pltpu.roll(sums[g * block : (g + 1) * block, LON_DEV:], g * PITCH, 1)
    east_ref[...] = east
    corner_ref[:block] = east
    corner_ref[block:] = east[:32]


def hot_rows(near_ref, far_ref, within, first, count):
    zero = jnp.zeros(near_ref.shape, BF16)
    hots = []
    for v in range(first, first + count):
        far_part = jnp.where(within == bf(v - 1), far_ref[...], zero) if v else zero
        hots.append(jnp.where(within == bf(v), near_ref[...], far_part))
    return jnp.concatenate(hots, axis=0)


def split_latitude(lat):
    group = jnp.floor(lat * (1.0 / SPAN))
    return group.astype(BF16), (lat - group * SPAN).astype(BF16)


def lower_kernel(x_ref, info_ref, acc_ref, near_ref, far_ref, left_ref, *, levels):
    rows, slots = x_ref.shape
    rest = levels % 8
    row = row_iota((LON_DEV, LANES)).astype(F32)
    for tile in range(slots // LANES):
        at = pl.ds(tile * LANES, LANES)
        w00, w01, w10, w11, _, lon = [info_ref[rest + i : rest + i + 1, at] for i in range(N_INFO)]
        here = row == lon
        after = row == lon + 1.0
        near_ref[:, at] = jnp.where(here, w00, jnp.where(after, w01, 0.0)).astype(BF16)
        far_ref[:, at] = jnp.where(here, w10, jnp.where(after, w11, 0.0)).astype(BF16)
    lat = info_ref[rest + 4 : rest + 5, :]
    group, within = split_latitude(lat)
    lat = lat.astype(BF16)
    x = x_ref[...]
    zero_x = jnp.zeros_like(x)
    for u in range(GROUPS):
        left_ref[u * rows : (u + 1) * rows, :] = jnp.where(group == bf(u), x, zero_x)
    zero = jnp.zeros((LON_DEV, slots), BF16)
    far = far_ref[...]
    hot = jnp.concatenate([jnp.where(lat == bf(SPAN * u - 1), far, zero) for u in range(1, GROUPS)], axis=0)
    seam = lax.dot_general(x, hot, NT, preferred_element_type=F32)
    for first in range(0, LOWER, 2):
        hot = hot_rows(near_ref, far_ref, within, first, 2)
        sums = lax.dot_general(left_ref[...], hot, NT, preferred_element_type=F32)
        for u in range(GROUPS):
            for i in range(2):
                value = sums[u * rows : (u + 1) * rows, i * LON_DEV : (i + 1) * LON_DEV]
                if first + i == 0 and u > 0:
                    value = value + seam[:, (u - 1) * LON_DEV : u * LON_DEV]
                acc_ref[u * LOWER + first + i] = value


def edge_column(fold, r, first_lane):
    parts = []
    for g in range(FOLD):
        shift = (LANES - g * PITCH - r) % LANES
        parts.append(pltpu.roll(fold, shift, 1) if shift else fold)
    return jnp.where(first_lane, jnp.concatenate(parts, axis=0), 0.0)


def upper_kernel(
    acc_ref, near_ref, far_ref, left_ref, info_ref, east_ref, out_hbm, south_ref, grid_ref, sems, *, levels
):
    rows = acc_ref.shape[1]
    rest = levels % 8
    first_lane = lane_iota((rows, LANES)) == 0
    copies = []

    def finish(r, value):
        value = value + edge_column(east_ref[...], r, first_lane)
        if r == 0:
            south_ref[...] = value
            return
        grid_ref[r] = value
        copy = pltpu.make_async_copy(grid_ref.at[r, 0:levels, :], out_hbm.at[:, r, :], sems.at[r])
        copy.start()
        copies.append(copy)

    for u in range(GROUPS):
        for v in range(LOWER):
            finish(u * SPAN + v, acc_ref[u * LOWER + v])
    _, within = split_latitude(info_ref[rest + 4 : rest + 5, :])
    for first in range(LOWER, SPAN, 2):
        hot = hot_rows(near_ref, far_ref, within, first, 2)
        sums = lax.dot_general(left_ref[...], hot, NT, preferred_element_type=F32)
        for u in range(GROUPS):
            for i in range(2):
                finish(
                    u * SPAN + first + i,
                    sums[u * rows : (u + 1) * rows, i * LON_DEV : (i + 1) * LON_DEV],
                )
    for copy in copies:
        copy.wait()


def last_kernel(south_ref, north_ref, corner_ref, grid_hbm, out_hbm, row_ref, sem):
    del grid_hbm
    first_lane = lane_iota(south_ref.shape) == 0
    passed = north_ref[...].astype(F32) + edge_column(corner_ref[: south_ref.shape[0] // FOLD], LAT_DEV, first_lane)
    row_ref[...] = south_ref[...] + jnp.where(lax.axis_index("band") > 0, passed, 0.0)
    copy = pltpu.make_async_copy(row_ref.at[0 : out_hbm.shape[0], :], out_hbm.at[:, 0, :], sem)
    copy.start()
    copy.wait()


def per_device(jacobian, departure, inv_var, frac, anchors, counts, *, n_band, n_lon):
    slots, levels = jacobian.shape
    devices = counts.shape[1]
    cap = slots // devices
    rows = -(-(levels + N_INFO) // 16) * 16
    half = rows // 2
    vmem = pl.BlockSpec(memory_space=pltpu.VMEM)
    hbm = pl.BlockSpec(memory_space=pltpu.HBM)
    params = pltpu.CompilerParams(vmem_limit_bytes=VMEM_LIMIT)
    struct = jax.ShapeDtypeStruct

    payload = pl.pallas_call(
        functools.partial(pack_kernel, cap=cap, lon_count=n_lon),
        out_shape=struct((devices, half, LANES), BF16),
        in_specs=[hbm] * 6,
        out_specs=hbm,
        scratch_shapes=[
            pltpu.VMEM((devices, half, LANES), BF16),
            pltpu.SMEM((1, devices), jnp.int32),
            pltpu.VMEM((levels, slots), BF16),
            pltpu.VMEM((1, slots), F32),
            pltpu.VMEM((1, slots), F32),
            pltpu.VMEM((2, slots), F32),
            pltpu.VMEM((2, slots), jnp.int32),
            pltpu.SemaphoreType.DMA((5 + 2 * JAC_CHUNKS,)),
        ],
        compiler_params=pltpu.CompilerParams(vmem_limit_bytes=VMEM_ALL),
        name="pack",
    )(counts, jacobian.T, departure[None, :], inv_var[None, :], frac, anchors)

    received = lax.all_to_all(payload, ("band", "lon"), split_axis=0, concat_axis=0, tiled=True)

    tail_rows = rows - levels // 8 * 8
    x, info, east, north, corner = pl.pallas_call(
        functools.partial(rim_kernel, cap=cap, levels=levels),
        out_shape=(
            struct((rows, slots), BF16),
            struct((tail_rows, slots), F32),
            struct((rows // FOLD, LANES), F32),
            struct((rows, LANES), BF16),
            struct((rows // FOLD + 32, LANES), F32),
        ),
        in_specs=[vmem],
        out_specs=(vmem,) * 5,
        scratch_shapes=[pltpu.VMEM((2 * LANES, slots), BF16)],
        compiler_params=params,
        name="rim",
    )(received)

    bands, lons = range(n_band), range(n_lon)
    north_in = lax.ppermute(north, "band", [(i, (i + 1) % n_band) for i in bands])
    corner_in = lax.ppermute(
        corner,
        ("band", "lon"),
        [(i * n_lon + j, (i + 1) % n_band * n_lon + (j + 1) % n_lon) for i in bands for j in lons],
    )
    east_in = lax.ppermute(east, "lon", [(j, (j + 1) % n_lon) for j in lons])

    acc, near, far, left = pl.pallas_call(
        functools.partial(lower_kernel, levels=levels),
        out_shape=(
            struct((GROUPS * LOWER, rows, LANES), F32),
            struct((LON_DEV, slots), BF16),
            struct((LON_DEV, slots), BF16),
            struct((GROUPS * rows, slots), BF16),
        ),
        in_specs=[vmem] * 2,
        out_specs=(vmem,) * 4,
        compiler_params=params,
        name="lower",
    )(x, info)

    grid, south = pl.pallas_call(
        functools.partial(upper_kernel, levels=levels),
        out_shape=(struct((levels, LAT_DEV, LON_DEV), F32), struct((rows, LANES), F32)),
        in_specs=[vmem] * 6,
        out_specs=(hbm, vmem),
        scratch_shapes=[pltpu.VMEM((LAT_DEV, rows, LANES), F32), pltpu.SemaphoreType.DMA((LAT_DEV,))],
        compiler_params=params,
        name="upper",
    )(acc, near, far, left, info, east_in)

    return pl.pallas_call(
        last_kernel,
        out_shape=struct((levels, LAT_DEV, LON_DEV), F32),
        in_specs=[vmem, vmem, vmem, hbm],
        out_specs=hbm,
        scratch_shapes=[pltpu.VMEM((rows, LANES), F32), pltpu.SemaphoreType.DMA],
        input_output_aliases={3: 0},
        compiler_params=params,
        name="last",
    )(south, north_in, corner_in, grid)


def solution(mesh):
    both = ("band", "lon")
    return jax.shard_map(
        functools.partial(per_device, n_band=mesh.shape["band"], n_lon=mesh.shape["lon"]),
        mesh=mesh,
        in_specs=(P(both, None), P(both), P(both), P(None, both), P(None, both), P(both, None)),
        out_specs=P(None, "band", "lon"),
        check_vma=False,
    )
```

```python
import functools

import jax
import jax.numpy as jnp
from jax import lax
from jax.experimental import pallas as pl
from jax.experimental.pallas import tpu as pltpu
from jax.sharding import PartitionSpec as P

LAT_DEV = 32
LON_DEV = 128
LANES = 128
N_INFO = 6
F32 = jnp.float32
BF16 = jnp.bfloat16
NT = (((1,), (1,)), ((), ()))
VMEM_LIMIT = 32 * 1024 * 1024
VMEM_ALL = 64 * 1024 * 1024
SPAN = 16
GROUPS = LAT_DEV // SPAN
LOWER = 12
EDGE_ROWS = -(-(LAT_DEV + 1) // 16) * 16
FOLD = 3
PITCH = LANES // FOLD
JAC_CHUNKS = 2


def bf(value):
    return jnp.asarray(value, F32).astype(BF16)


def lane_iota(shape):
    return lax.broadcasted_iota(jnp.int32, shape, len(shape) - 1)


def row_iota(shape):
    return lax.broadcasted_iota(jnp.int32, shape, 0)


def swap_halves(first, second, cap):
    low = lane_iota(first.shape) < cap
    return (
        jnp.where(low, first, pltpu.roll(second, cap, 1)),
        jnp.where(low, pltpu.roll(first, cap, 1), second),
    )


def pack_kernel(
    counts_hbm, jac_hbm, dep_hbm, inv_hbm, frac_hbm, anchor_hbm, out_hbm,
    out_ref, counts_ref, jac_ref, dep_ref, inv_ref, frac_ref, anchor_ref, sems, *, cap, lon_count,
):
    levels, slots = jac_ref.shape
    half = out_ref.shape[1]
    body = (levels // 8) * 8
    rest = levels - body
    small = [
        pltpu.make_async_copy(src, dst, sems.at[i])
        for i, (src, dst) in enumerate(
            [
                (counts_hbm, counts_ref),
                (dep_hbm, dep_ref),
                (inv_hbm, inv_ref),
                (frac_hbm, frac_ref),
                (anchor_hbm, anchor_ref),
            ]
        )
    ]
    chunk = slots // JAC_CHUNKS
    large = [
        pltpu.make_async_copy(
            jac_hbm.at[:, pl.ds(i * chunk, chunk)],
            jac_ref.at[:, pl.ds(i * chunk, chunk)],
            sems.at[len(small) + i],
        )
        for i in range(JAC_CHUNKS)
    ]
    for copy in large + small:
        copy.start()
    for copy in small:
        copy.wait()
    stores = []
    lane = lane_iota((1, LANES))
    low = lane < cap
    for tile in range(slots // LANES):
        if tile * LANES % chunk == 0:
            large[tile * LANES // chunk].wait()
        at = pl.ds(tile * LANES, LANES)
        first, second = 2 * tile, 2 * tile + 1
        count = jnp.where(low, counts_ref[0, first], counts_ref[0, second] + cap)
        live = lane < count
        forcing = jnp.where(live, dep_ref[:, at] * inv_ref[:, at], 0.0)
        a = frac_ref[0:1, at]
        b = frac_ref[1:2, at]
        lat0 = jnp.where(low, first // lon_count * LAT_DEV, second // lon_count * LAT_DEV)
        lon0 = jnp.where(low, first % lon_count * LON_DEV, second % lon_count * LON_DEV)
        info = [
            (1.0 - a) * (1.0 - b),
            (1.0 - a) * b,
            a * (1.0 - b),
            a * b,
            (anchor_ref[0:1, at] - lat0).astype(F32),
            (anchor_ref[1:2, at] - lon0).astype(F32),
        ]
        adjoint = jac_ref[0:body, at].astype(F32) * forcing
        tail_rows = 2 * half - body
        tail = jnp.zeros((tail_rows, LANES), F32)
        row = row_iota((tail_rows, LANES))
        for i in range(rest):
            tail = jnp.where(row == i, jac_ref[body + i : body + i + 1, at].astype(F32) * forcing, tail)
        for i, value in enumerate(info):
            tail = jnp.where(row == rest + i, jnp.where(live, value, 0.0), tail)
        whole = jnp.concatenate([adjoint, tail], axis=0)
        one, two = swap_halves(whole[:half], whole[half:], cap)
        out_ref[first] = one.astype(BF16)
        out_ref[second] = two.astype(BF16)
        if (tile + 1) * LANES % chunk == 0:
            done = tile * LANES // chunk
            part = pl.ds(done * chunk // cap, chunk // cap)
            copy = pltpu.make_async_copy(out_ref.at[part], out_hbm.at[part], sems.at[len(small) + JAC_CHUNKS + done])
            copy.start()
            stores.append(copy)
    for copy in stores:
        copy.wait()


def rim_kernel(recv_ref, x_ref, info_ref, east_ref, north_ref, corner_ref, hot_ref, *, cap, levels):
    devices, half, _ = recv_ref.shape
    body = (levels // 8) * 8
    rest = levels - body
    row = row_iota((LON_DEV, LANES)).astype(F32)
    for tile in range(devices // 2):
        at = pl.ds(tile * LANES, LANES)
        low, high = swap_halves(recv_ref[2 * tile].astype(F32), recv_ref[2 * tile + 1].astype(F32), cap)
        whole = jnp.concatenate([low, high], axis=0)
        x_ref[:, at] = whole.astype(BF16)
        info = whole[body:]
        info_ref[:, at] = info
        w01, w10, w11, lat, lon = [info[rest + i : rest + i + 1] for i in range(1, N_INFO)]
        top = lat == LAT_DEV - 1.0
        w10 = jnp.where(top, w10, 0.0)
        w11_top = jnp.where(top, w11, 0.0)
        hot_ref[0:LON_DEV, at] = jnp.where(
            row == lon, w10, jnp.where(row == lon + 1.0, w11_top, 0.0)
        ).astype(BF16)
        edge = lon == LON_DEV - 1.0
        w01 = jnp.where(edge, w01, 0.0)
        w11 = jnp.where(edge, w11, 0.0)
        few = row[:EDGE_ROWS]
        hot_ref[LON_DEV : LON_DEV + EDGE_ROWS, at] = jnp.where(
            few == lat, w01, jnp.where(few == lat + 1.0, w11, 0.0)
        ).astype(BF16)
    hot_ref[LON_DEV + EDGE_ROWS :, :] = jnp.zeros((LANES - EDGE_ROWS, x_ref.shape[1]), BF16)
    sums = lax.dot_general(x_ref[...], hot_ref[...], NT, preferred_element_type=F32)
    north_ref[...] = sums[:, :LON_DEV].astype(BF16)
    block = east_ref.shape[0]
    east = sums[:block, LON_DEV:]
    for g in range(1, FOLD):
        east = east + pltpu.roll(sums[g * block : (g + 1) * block, LON_DEV:], g * PITCH, 1)
    east_ref[...] = east
    corner_ref[:block] = east
    corner_ref[block:] = east[:32]


def hot_rows(near_ref, far_ref, within, first, count):
    zero = jnp.zeros(near_ref.shape, BF16)
    hots = []
    for v in range(first, first + count):
        far_part = jnp.where(within == bf(v - 1), far_ref[...], zero) if v else zero
        hots.append(jnp.where(within == bf(v), near_ref[...], far_part))
    return jnp.concatenate(hots, axis=0)


def split_latitude(lat):
    group = jnp.floor(lat * (1.0 / SPAN))
    return group.astype(BF16), (lat - group * SPAN).astype(BF16)


def lower_kernel(x_ref, info_ref, acc_ref, near_ref, far_ref, left_ref, *, levels):
    rows, slots = x_ref.shape
    rest = levels % 8
    row = row_iota((LON_DEV, LANES)).astype(F32)
    for tile in range(slots // LANES):
        at = pl.ds(tile * LANES, LANES)
        w00, w01, w10, w11, _, lon = [info_ref[rest + i : rest + i + 1, at] for i in range(N_INFO)]
        here = row == lon
        after = row == lon + 1.0
        near_ref[:, at] = jnp.where(here, w00, jnp.where(after, w01, 0.0)).astype(BF16)
        far_ref[:, at] = jnp.where(here, w10, jnp.where(after, w11, 0.0)).astype(BF16)
    lat = info_ref[rest + 4 : rest + 5, :]
    group, within = split_latitude(lat)
    lat = lat.astype(BF16)
    x = x_ref[...]
    zero_x = jnp.zeros_like(x)
    for u in range(GROUPS):
        left_ref[u * rows : (u + 1) * rows, :] = jnp.where(group == bf(u), x, zero_x)
    zero = jnp.zeros((LON_DEV, slots), BF16)
    far = far_ref[...]
    hot = jnp.concatenate([jnp.where(lat == bf(SPAN * u - 1), far, zero) for u in range(1, GROUPS)], axis=0)
    seam = lax.dot_general(x, hot, NT, preferred_element_type=F32)
    for first in range(0, LOWER, 2):
        hot = hot_rows(near_ref, far_ref, within, first, 2)
        sums = lax.dot_general(left_ref[...], hot, NT, preferred_element_type=F32)
        for u in range(GROUPS):
            for i in range(2):
                value = sums[u * rows : (u + 1) * rows, i * LON_DEV : (i + 1) * LON_DEV]
                if first + i == 0 and u > 0:
                    value = value + seam[:, (u - 1) * LON_DEV : u * LON_DEV]
                acc_ref[u * LOWER + first + i] = value


def edge_column(fold, r, first_lane):
    parts = []
    for g in range(FOLD):
        shift = (LANES - g * PITCH - r) % LANES
        parts.append(pltpu.roll(fold, shift, 1) if shift else fold)
    return jnp.where(first_lane, jnp.concatenate(parts, axis=0), 0.0)


def upper_kernel(
    acc_ref, near_ref, far_ref, left_ref, info_ref, east_ref, out_hbm, south_ref, grid_ref, sems, *, levels
):
    rows = acc_ref.shape[1]
    rest = levels % 8
    first_lane = lane_iota((rows, LANES)) == 0
    copies = []

    def finish(r, value):
        value = value + edge_column(east_ref[...], r, first_lane)
        if r == 0:
            south_ref[...] = value
            return
        grid_ref[r] = value
        copy = pltpu.make_async_copy(grid_ref.at[r, 0:levels, :], out_hbm.at[:, r, :], sems.at[r])
        copy.start()
        copies.append(copy)

    for u in range(GROUPS):
        for v in range(LOWER):
            finish(u * SPAN + v, acc_ref[u * LOWER + v])
    _, within = split_latitude(info_ref[rest + 4 : rest + 5, :])
    for first in range(LOWER, SPAN, 2):
        hot = hot_rows(near_ref, far_ref, within, first, 2)
        sums = lax.dot_general(left_ref[...], hot, NT, preferred_element_type=F32)
        for u in range(GROUPS):
            for i in range(2):
                finish(
                    u * SPAN + first + i,
                    sums[u * rows : (u + 1) * rows, i * LON_DEV : (i + 1) * LON_DEV],
                )
    for copy in copies:
        copy.wait()


def last_kernel(south_ref, north_ref, corner_ref, grid_hbm, out_hbm, row_ref, sem):
    del grid_hbm
    first_lane = lane_iota(south_ref.shape) == 0
    passed = north_ref[...].astype(F32) + edge_column(corner_ref[: south_ref.shape[0] // FOLD], LAT_DEV, first_lane)
    row_ref[...] = south_ref[...] + jnp.where(lax.axis_index("band") > 0, passed, 0.0)
    copy = pltpu.make_async_copy(row_ref.at[0 : out_hbm.shape[0], :], out_hbm.at[:, 0, :], sem)
    copy.start()
    copy.wait()


def per_device(jacobian, departure, inv_var, frac, anchors, counts, *, n_band, n_lon):
    slots, levels = jacobian.shape
    devices = counts.shape[1]
    cap = slots // devices
    rows = -(-(levels + N_INFO) // 16) * 16
    half = rows // 2
    vmem = pl.BlockSpec(memory_space=pltpu.VMEM)
    hbm = pl.BlockSpec(memory_space=pltpu.HBM)
    params = pltpu.CompilerParams(vmem_limit_bytes=VMEM_LIMIT)
    struct = jax.ShapeDtypeStruct

    payload = pl.pallas_call(
        functools.partial(pack_kernel, cap=cap, lon_count=n_lon),
        out_shape=struct((devices, half, LANES), BF16),
        in_specs=[hbm] * 6,
        out_specs=hbm,
        scratch_shapes=[
            pltpu.VMEM((devices, half, LANES), BF16),
            pltpu.SMEM((1, devices), jnp.int32),
            pltpu.VMEM((levels, slots), BF16),
            pltpu.VMEM((1, slots), F32),
            pltpu.VMEM((1, slots), F32),
            pltpu.VMEM((2, slots), F32),
            pltpu.VMEM((2, slots), jnp.int32),
            pltpu.SemaphoreType.DMA((5 + 2 * JAC_CHUNKS,)),
        ],
        compiler_params=pltpu.CompilerParams(vmem_limit_bytes=VMEM_ALL),
        name="pack",
    )(counts, jacobian.T, departure[None, :], inv_var[None, :], frac, anchors)

    received = lax.all_to_all(payload, ("band", "lon"), split_axis=0, concat_axis=0, tiled=True)

    tail_rows = rows - levels // 8 * 8
    x, info, east, north, corner = pl.pallas_call(
        functools.partial(rim_kernel, cap=cap, levels=levels),
        out_shape=(
            struct((rows, slots), BF16),
            struct((tail_rows, slots), F32),
            struct((rows // FOLD, LANES), F32),
            struct((rows, LANES), BF16),
            struct((rows // FOLD + 32, LANES), F32),
        ),
        in_specs=[vmem],
        out_specs=(vmem,) * 5,
        scratch_shapes=[pltpu.VMEM((2 * LANES, slots), BF16)],
        compiler_params=params,
        name="rim",
    )(received)

    bands, lons = range(n_band), range(n_lon)
    north_in = lax.ppermute(north, "band", [(i, (i + 1) % n_band) for i in bands])
    corner_in = lax.ppermute(
        corner,
        ("band", "lon"),
        [
            (i * n_lon + j, (i + 1) % n_band * n_lon + (j + (i + 1 < n_band)) % n_lon)
            for i in bands
            for j in lons
        ],
    )
    east_in = lax.ppermute(east, "lon", [(j, (j + 1) % n_lon) for j in lons])

    acc, near, far, left = pl.pallas_call(
        functools.partial(lower_kernel, levels=levels),
        out_shape=(
            struct((GROUPS * LOWER, rows, LANES), F32),
            struct((LON_DEV, slots), BF16),
            struct((LON_DEV, slots), BF16),
            struct((GROUPS * rows, slots), BF16),
        ),
        in_specs=[vmem] * 2,
        out_specs=(vmem,) * 4,
        compiler_params=params,
        name="lower",
    )(x, info)

    grid, south = pl.pallas_call(
        functools.partial(upper_kernel, levels=levels),
        out_shape=(struct((levels, LAT_DEV, LON_DEV), F32), struct((rows, LANES), F32)),
        in_specs=[vmem] * 6,
        out_specs=(hbm, vmem),
        scratch_shapes=[pltpu.VMEM((LAT_DEV, rows, LANES), F32), pltpu.SemaphoreType.DMA((LAT_DEV,))],
        compiler_params=params,
        name="upper",
    )(acc, near, far, left, info, east_in)

    return pl.pallas_call(
        last_kernel,
        out_shape=struct((levels, LAT_DEV, LON_DEV), F32),
        in_specs=[vmem, vmem, vmem, hbm],
        out_specs=hbm,
        scratch_shapes=[pltpu.VMEM((rows, LANES), F32), pltpu.SemaphoreType.DMA],
        input_output_aliases={3: 0},
        compiler_params=params,
        name="last",
    )(south, north_in, corner_in, grid)


def solution(mesh):
    both = ("band", "lon")
    return jax.shard_map(
        functools.partial(per_device, n_band=mesh.shape["band"], n_lon=mesh.shape["lon"]),
        mesh=mesh,
        in_specs=(P(both, None), P(both), P(both), P(None, both), P(None, both), P(both, None)),
        out_specs=P(None, "band", "lon"),
        check_vma=False,
    )
```

```python
import functools

import jax
import jax.numpy as jnp
from jax import lax
from jax.experimental import pallas as pl
from jax.experimental.pallas import tpu as pltpu
from jax.sharding import PartitionSpec as P

LAT_DEV = 32
LON_DEV = 128
LANES = 128
N_INFO = 6
F32 = jnp.float32
BF16 = jnp.bfloat16
NT = (((1,), (1,)), ((), ()))
VMEM_LIMIT = 32 * 1024 * 1024
VMEM_ALL = 64 * 1024 * 1024
SPAN = 16
GROUPS = LAT_DEV // SPAN
LOWER = 12
EDGE_ROWS = -(-(LAT_DEV + 1) // 16) * 16
FOLD = 3
OUT_CHUNKS = 4
PITCH = LANES // FOLD
JAC_CHUNKS = 2


def bf(value):
    return jnp.asarray(value, F32).astype(BF16)


def lane_iota(shape):
    return lax.broadcasted_iota(jnp.int32, shape, len(shape) - 1)


def row_iota(shape):
    return lax.broadcasted_iota(jnp.int32, shape, 0)


def swap_halves(first, second, cap):
    low = lane_iota(first.shape) < cap
    return (
        jnp.where(low, first, pltpu.roll(second, cap, 1)),
        jnp.where(low, pltpu.roll(first, cap, 1), second),
    )


def pack_kernel(
    counts_hbm, jac_hbm, dep_hbm, inv_hbm, frac_hbm, anchor_hbm, out_hbm,
    out_ref, counts_ref, jac_ref, dep_ref, inv_ref, frac_ref, anchor_ref, sems, *, cap, lon_count,
):
    levels, slots = jac_ref.shape
    half = out_ref.shape[1]
    body = (levels // 8) * 8
    rest = levels - body
    small = [
        pltpu.make_async_copy(src, dst, sems.at[i])
        for i, (src, dst) in enumerate(
            [
                (counts_hbm, counts_ref),
                (dep_hbm, dep_ref),
                (inv_hbm, inv_ref),
                (frac_hbm, frac_ref),
                (anchor_hbm, anchor_ref),
            ]
        )
    ]
    chunk = slots // JAC_CHUNKS
    large = [
        pltpu.make_async_copy(
            jac_hbm.at[:, pl.ds(i * chunk, chunk)],
            jac_ref.at[:, pl.ds(i * chunk, chunk)],
            sems.at[len(small) + i],
        )
        for i in range(JAC_CHUNKS)
    ]
    for copy in large + small:
        copy.start()
    for copy in small:
        copy.wait()
    stores = []
    piece = slots // OUT_CHUNKS
    lane = lane_iota((1, LANES))
    low = lane < cap
    for tile in range(slots // LANES):
        if tile * LANES % chunk == 0:
            large[tile * LANES // chunk].wait()
        at = pl.ds(tile * LANES, LANES)
        first, second = 2 * tile, 2 * tile + 1
        count = jnp.where(low, counts_ref[0, first], counts_ref[0, second] + cap)
        live = lane < count
        forcing = jnp.where(live, dep_ref[:, at] * inv_ref[:, at], 0.0)
        a = frac_ref[0:1, at]
        b = frac_ref[1:2, at]
        lat0 = jnp.where(low, first // lon_count * LAT_DEV, second // lon_count * LAT_DEV)
        lon0 = jnp.where(low, first % lon_count * LON_DEV, second % lon_count * LON_DEV)
        info = [
            (1.0 - a) * (1.0 - b),
            (1.0 - a) * b,
            a * (1.0 - b),
            a * b,
            (anchor_ref[0:1, at] - lat0).astype(F32),
            (anchor_ref[1:2, at] - lon0).astype(F32),
        ]
        adjoint = jac_ref[0:body, at].astype(F32) * forcing
        tail_rows = 2 * half - body
        tail = jnp.zeros((tail_rows, LANES), F32)
        row = row_iota((tail_rows, LANES))
        for i in range(rest):
            tail = jnp.where(row == i, jac_ref[body + i : body + i + 1, at].astype(F32) * forcing, tail)
        for i, value in enumerate(info):
            tail = jnp.where(row == rest + i, jnp.where(live, value, 0.0), tail)
        whole = jnp.concatenate([adjoint, tail], axis=0)
        one, two = swap_halves(whole[:half], whole[half:], cap)
        out_ref[first] = one.astype(BF16)
        out_ref[second] = two.astype(BF16)
        if (tile + 1) * LANES % piece == 0:
            done = tile * LANES // piece
            part = pl.ds(done * piece // cap, piece // cap)
            copy = pltpu.make_async_copy(out_ref.at[part], out_hbm.at[part], sems.at[len(small) + JAC_CHUNKS + done])
            copy.start()
            stores.append(copy)
    for copy in stores:
        copy.wait()


def rim_kernel(recv_ref, x_ref, info_ref, east_ref, north_ref, corner_ref, hot_ref, *, cap, levels):
    devices, half, _ = recv_ref.shape
    body = (levels // 8) * 8
    rest = levels - body
    row = row_iota((LON_DEV, LANES)).astype(F32)
    for tile in range(devices // 2):
        at = pl.ds(tile * LANES, LANES)
        low, high = swap_halves(recv_ref[2 * tile].astype(F32), recv_ref[2 * tile + 1].astype(F32), cap)
        whole = jnp.concatenate([low, high], axis=0)
        x_ref[:, at] = whole.astype(BF16)
        info = whole[body:]
        info_ref[:, at] = info
        w01, w10, w11, lat, lon = [info[rest + i : rest + i + 1] for i in range(1, N_INFO)]
        top = lat == LAT_DEV - 1.0
        w10 = jnp.where(top, w10, 0.0)
        w11_top = jnp.where(top, w11, 0.0)
        hot_ref[0:LON_DEV, at] = jnp.where(
            row == lon, w10, jnp.where(row == lon + 1.0, w11_top, 0.0)
        ).astype(BF16)
        edge = lon == LON_DEV - 1.0
        w01 = jnp.where(edge, w01, 0.0)
        w11 = jnp.where(edge, w11, 0.0)
        few = row[:EDGE_ROWS]
        hot_ref[LON_DEV : LON_DEV + EDGE_ROWS, at] = jnp.where(
            few == lat, w01, jnp.where(few == lat + 1.0, w11, 0.0)
        ).astype(BF16)
    hot_ref[LON_DEV + EDGE_ROWS :, :] = jnp.zeros((LANES - EDGE_ROWS, x_ref.shape[1]), BF16)
    sums = lax.dot_general(x_ref[...], hot_ref[...], NT, preferred_element_type=F32)
    north_ref[...] = sums[:, :LON_DEV].astype(BF16)
    block = east_ref.shape[0]
    east = sums[:block, LON_DEV:]
    for g in range(1, FOLD):
        east = east + pltpu.roll(sums[g * block : (g + 1) * block, LON_DEV:], g * PITCH, 1)
    east_ref[...] = east
    corner_ref[:block] = east
    corner_ref[block:] = east[:32]


def hot_rows(near_ref, far_ref, within, first, count):
    zero = jnp.zeros(near_ref.shape, BF16)
    hots = []
    for v in range(first, first + count):
        far_part = jnp.where(within == bf(v - 1), far_ref[...], zero) if v else zero
        hots.append(jnp.where(within == bf(v), near_ref[...], far_part))
    return jnp.concatenate(hots, axis=0)


def split_latitude(lat):
    group = jnp.floor(lat * (1.0 / SPAN))
    return group.astype(BF16), (lat - group * SPAN).astype(BF16)


def lower_kernel(x_ref, info_ref, acc_ref, near_ref, far_ref, left_ref, *, levels):
    rows, slots = x_ref.shape
    rest = levels % 8
    row = row_iota((LON_DEV, LANES)).astype(F32)
    for tile in range(slots // LANES):
        at = pl.ds(tile * LANES, LANES)
        w00, w01, w10, w11, _, lon = [info_ref[rest + i : rest + i + 1, at] for i in range(N_INFO)]
        here = row == lon
        after = row == lon + 1.0
        near_ref[:, at] = jnp.where(here, w00, jnp.where(after, w01, 0.0)).astype(BF16)
        far_ref[:, at] = jnp.where(here, w10, jnp.where(after, w11, 0.0)).astype(BF16)
    lat = info_ref[rest + 4 : rest + 5, :]
    group, within = split_latitude(lat)
    lat = lat.astype(BF16)
    x = x_ref[...]
    zero_x = jnp.zeros_like(x)
    for u in range(GROUPS):
        left_ref[u * rows : (u + 1) * rows, :] = jnp.where(group == bf(u), x, zero_x)
    zero = jnp.zeros((LON_DEV, slots), BF16)
    far = far_ref[...]
    hot = jnp.concatenate([jnp.where(lat == bf(SPAN * u - 1), far, zero) for u in range(1, GROUPS)], axis=0)
    seam = lax.dot_general(x, hot, NT, preferred_element_type=F32)
    for first in range(0, LOWER, 2):
        hot = hot_rows(near_ref, far_ref, within, first, 2)
        sums = lax.dot_general(left_ref[...], hot, NT, preferred_element_type=F32)
        for u in range(GROUPS):
            for i in range(2):
                value = sums[u * rows : (u + 1) * rows, i * LON_DEV : (i + 1) * LON_DEV]
                if first + i == 0 and u > 0:
                    value = value + seam[:, (u - 1) * LON_DEV : u * LON_DEV]
                acc_ref[u * LOWER + first + i] = value


def edge_column(fold, r, first_lane):
    parts = []
    for g in range(FOLD):
        shift = (LANES - g * PITCH - r) % LANES
        parts.append(pltpu.roll(fold, shift, 1) if shift else fold)
    return jnp.where(first_lane, jnp.concatenate(parts, axis=0), 0.0)


def upper_kernel(
    acc_ref, near_ref, far_ref, left_ref, info_ref, east_ref, out_hbm, south_ref, grid_ref, sems, *, levels
):
    rows = acc_ref.shape[1]
    rest = levels % 8
    first_lane = lane_iota((rows, LANES)) == 0
    copies = []

    def finish(r, value):
        value = value + edge_column(east_ref[...], r, first_lane)
        if r == 0:
            south_ref[...] = value
            return
        grid_ref[r] = value
        copy = pltpu.make_async_copy(grid_ref.at[r, 0:levels, :], out_hbm.at[:, r, :], sems.at[r])
        copy.start()
        copies.append(copy)

    for u in range(GROUPS):
        for v in range(LOWER):
            finish(u * SPAN + v, acc_ref[u * LOWER + v])
    _, within = split_latitude(info_ref[rest + 4 : rest + 5, :])
    for first in range(LOWER, SPAN, 2):
        hot = hot_rows(near_ref, far_ref, within, first, 2)
        sums = lax.dot_general(left_ref[...], hot, NT, preferred_element_type=F32)
        for u in range(GROUPS):
            for i in range(2):
                finish(
                    u * SPAN + first + i,
                    sums[u * rows : (u + 1) * rows, i * LON_DEV : (i + 1) * LON_DEV],
                )
    for copy in copies:
        copy.wait()


def last_kernel(south_ref, north_ref, corner_ref, grid_hbm, out_hbm, row_ref, sem):
    del grid_hbm
    first_lane = lane_iota(south_ref.shape) == 0
    passed = north_ref[...].astype(F32) + edge_column(corner_ref[: south_ref.shape[0] // FOLD], LAT_DEV, first_lane)
    row_ref[...] = south_ref[...] + jnp.where(lax.axis_index("band") > 0, passed, 0.0)
    copy = pltpu.make_async_copy(row_ref.at[0 : out_hbm.shape[0], :], out_hbm.at[:, 0, :], sem)
    copy.start()
    copy.wait()


def per_device(jacobian, departure, inv_var, frac, anchors, counts, *, n_band, n_lon):
    slots, levels = jacobian.shape
    devices = counts.shape[1]
    cap = slots // devices
    rows = -(-(levels + N_INFO) // 16) * 16
    half = rows // 2
    vmem = pl.BlockSpec(memory_space=pltpu.VMEM)
    hbm = pl.BlockSpec(memory_space=pltpu.HBM)
    params = pltpu.CompilerParams(vmem_limit_bytes=VMEM_LIMIT)
    struct = jax.ShapeDtypeStruct

    payload = pl.pallas_call(
        functools.partial(pack_kernel, cap=cap, lon_count=n_lon),
        out_shape=struct((devices, half, LANES), BF16),
        in_specs=[hbm] * 6,
        out_specs=hbm,
        scratch_shapes=[
            pltpu.VMEM((devices, half, LANES), BF16),
            pltpu.SMEM((1, devices), jnp.int32),
            pltpu.VMEM((levels, slots), BF16),
            pltpu.VMEM((1, slots), F32),
            pltpu.VMEM((1, slots), F32),
            pltpu.VMEM((2, slots), F32),
            pltpu.VMEM((2, slots), jnp.int32),
            pltpu.SemaphoreType.DMA((5 + JAC_CHUNKS + OUT_CHUNKS,)),
        ],
        compiler_params=pltpu.CompilerParams(vmem_limit_bytes=VMEM_ALL),
        name="pack",
    )(counts, jacobian.T, departure[None, :], inv_var[None, :], frac, anchors)

    received = lax.all_to_all(payload, ("band", "lon"), split_axis=0, concat_axis=0, tiled=True)

    tail_rows = rows - levels // 8 * 8
    x, info, east, north, corner = pl.pallas_call(
        functools.partial(rim_kernel, cap=cap, levels=levels),
        out_shape=(
            struct((rows, slots), BF16),
            struct((tail_rows, slots), F32),
            struct((rows // FOLD, LANES), F32),
            struct((rows, LANES), BF16),
            struct((rows // FOLD + 32, LANES), F32),
        ),
        in_specs=[vmem],
        out_specs=(vmem,) * 5,
        scratch_shapes=[pltpu.VMEM((2 * LANES, slots), BF16)],
        compiler_params=params,
        name="rim",
    )(received)

    bands, lons = range(n_band), range(n_lon)
    north_in = lax.ppermute(north, "band", [(i, (i + 1) % n_band) for i in bands])
    corner_in = lax.ppermute(
        corner,
        ("band", "lon"),
        [
            (i * n_lon + j, (i + 1) % n_band * n_lon + (j + (i + 1 < n_band)) % n_lon)
            for i in bands
            for j in lons
        ],
    )
    east_in = lax.ppermute(east, "lon", [(j, (j + 1) % n_lon) for j in lons])

    acc, near, far, left = pl.pallas_call(
        functools.partial(lower_kernel, levels=levels),
        out_shape=(
            struct((GROUPS * LOWER, rows, LANES), F32),
            struct((LON_DEV, slots), BF16),
            struct((LON_DEV, slots), BF16),
            struct((GROUPS * rows, slots), BF16),
        ),
        in_specs=[vmem] * 2,
        out_specs=(vmem,) * 4,
        compiler_params=params,
        name="lower",
    )(x, info)

    grid, south = pl.pallas_call(
        functools.partial(upper_kernel, levels=levels),
        out_shape=(struct((levels, LAT_DEV, LON_DEV), F32), struct((rows, LANES), F32)),
        in_specs=[vmem] * 6,
        out_specs=(hbm, vmem),
        scratch_shapes=[pltpu.VMEM((LAT_DEV, rows, LANES), F32), pltpu.SemaphoreType.DMA((LAT_DEV,))],
        compiler_params=params,
        name="upper",
    )(acc, near, far, left, info, east_in)

    return pl.pallas_call(
        last_kernel,
        out_shape=struct((levels, LAT_DEV, LON_DEV), F32),
        in_specs=[vmem, vmem, vmem, hbm],
        out_specs=hbm,
        scratch_shapes=[pltpu.VMEM((rows, LANES), F32), pltpu.SemaphoreType.DMA],
        input_output_aliases={3: 0},
        compiler_params=params,
        name="last",
    )(south, north_in, corner_in, grid)


def solution(mesh):
    both = ("band", "lon")
    return jax.shard_map(
        functools.partial(per_device, n_band=mesh.shape["band"], n_lon=mesh.shape["lon"]),
        mesh=mesh,
        in_specs=(P(both, None), P(both), P(both), P(None, both), P(None, both), P(both, None)),
        out_specs=P(None, "band", "lon"),
        check_vma=False,
    )
```

```python
import functools

import jax
import jax.numpy as jnp
from jax import lax
from jax.experimental import pallas as pl
from jax.experimental.pallas import tpu as pltpu
from jax.sharding import PartitionSpec as P

LAT_DEV = 32
LON_DEV = 128
LANES = 128
N_INFO = 6
F32 = jnp.float32
BF16 = jnp.bfloat16
NT = (((1,), (1,)), ((), ()))
VMEM_LIMIT = 32 * 1024 * 1024
VMEM_ALL = 64 * 1024 * 1024
SPAN = 16
GROUPS = LAT_DEV // SPAN
LOWER = 12
EDGE_ROWS = -(-(LAT_DEV + 1) // 16) * 16
FOLD = 3
OUT_CHUNKS = 4
PITCH = LANES // FOLD
JAC_CHUNKS = 2


def bf(value):
    return jnp.asarray(value, F32).astype(BF16)


def lane_iota(shape):
    return lax.broadcasted_iota(jnp.int32, shape, len(shape) - 1)


def row_iota(shape):
    return lax.broadcasted_iota(jnp.int32, shape, 0)


def swap_halves(first, second, cap):
    low = lane_iota(first.shape) < cap
    return (
        jnp.where(low, first, pltpu.roll(second, cap, 1)),
        jnp.where(low, pltpu.roll(first, cap, 1), second),
    )


def pack_kernel(
    counts_hbm, jac_hbm, dep_hbm, inv_hbm, frac_hbm, anchor_hbm, out_hbm,
    out_ref, counts_ref, jac_ref, dep_ref, inv_ref, frac_ref, anchor_ref, sems, *, cap, lon_count,
):
    levels, slots = jac_ref.shape
    half = out_ref.shape[1]
    body = (levels // 8) * 8
    rest = levels - body
    small = [
        pltpu.make_async_copy(src, dst, sems.at[i])
        for i, (src, dst) in enumerate(
            [
                (counts_hbm, counts_ref),
                (dep_hbm, dep_ref),
                (inv_hbm, inv_ref),
                (frac_hbm, frac_ref),
                (anchor_hbm, anchor_ref),
            ]
        )
    ]
    chunk = slots // JAC_CHUNKS
    large = [
        pltpu.make_async_copy(
            jac_hbm.at[:, pl.ds(i * chunk, chunk)],
            jac_ref.at[:, pl.ds(i * chunk, chunk)],
            sems.at[len(small) + i],
        )
        for i in range(JAC_CHUNKS)
    ]
    for copy in large + small:
        copy.start()
    for copy in small:
        copy.wait()
    stores = []
    piece = slots // OUT_CHUNKS
    lane = lane_iota((1, LANES))
    low = lane < cap
    for tile in range(slots // LANES):
        if tile * LANES % chunk == 0:
            large[tile * LANES // chunk].wait()
        at = pl.ds(tile * LANES, LANES)
        first, second = 2 * tile, 2 * tile + 1
        count = jnp.where(low, counts_ref[0, first], counts_ref[0, second] + cap)
        live = lane < count
        forcing = jnp.where(live, dep_ref[:, at] * inv_ref[:, at], 0.0)
        a = frac_ref[0:1, at]
        b = frac_ref[1:2, at]
        lat0 = jnp.where(low, first // lon_count * LAT_DEV, second // lon_count * LAT_DEV)
        lon0 = jnp.where(low, first % lon_count * LON_DEV, second % lon_count * LON_DEV)
        info = [
            (1.0 - a) * (1.0 - b),
            (1.0 - a) * b,
            a * (1.0 - b),
            a * b,
            (anchor_ref[0:1, at] - lat0).astype(F32),
            (anchor_ref[1:2, at] - lon0).astype(F32),
        ]
        adjoint = jac_ref[0:body, at].astype(F32) * forcing
        tail_rows = 2 * half - body
        tail = jnp.zeros((tail_rows, LANES), F32)
        row = row_iota((tail_rows, LANES))
        for i in range(rest):
            tail = jnp.where(row == i, jac_ref[body + i : body + i + 1, at].astype(F32) * forcing, tail)
        for i, value in enumerate(info):
            tail = jnp.where(row == rest + i, jnp.where(live, value, 0.0), tail)
        whole = jnp.concatenate([adjoint, tail], axis=0)
        one, two = swap_halves(whole[:half], whole[half:], cap)
        out_ref[first] = one.astype(BF16)
        out_ref[second] = two.astype(BF16)
        if (tile + 1) * LANES % piece == 0:
            done = tile * LANES // piece
            part = pl.ds(done * piece // cap, piece // cap)
            copy = pltpu.make_async_copy(out_ref.at[part], out_hbm.at[part], sems.at[len(small) + JAC_CHUNKS + done])
            copy.start()
            stores.append(copy)
    for copy in stores:
        copy.wait()


def rim_kernel(recv_ref, x_ref, info_ref, east_ref, north_ref, corner_ref, hot_ref, *, cap, levels):
    devices, half, _ = recv_ref.shape
    body = (levels // 8) * 8
    rest = levels - body
    row = row_iota((LON_DEV, LANES)).astype(F32)
    for tile in range(devices // 2):
        at = pl.ds(tile * LANES, LANES)
        low, high = swap_halves(recv_ref[2 * tile].astype(F32), recv_ref[2 * tile + 1].astype(F32), cap)
        whole = jnp.concatenate([low, high], axis=0)
        x_ref[:, at] = whole.astype(BF16)
        info = whole[body:]
        info_ref[:, at] = info
        w01, w10, w11, lat, lon = [info[rest + i : rest + i + 1] for i in range(1, N_INFO)]
        top = lat == LAT_DEV - 1.0
        w10 = jnp.where(top, w10, 0.0)
        w11_top = jnp.where(top, w11, 0.0)
        hot_ref[0:LON_DEV, at] = jnp.where(
            row == lon, w10, jnp.where(row == lon + 1.0, w11_top, 0.0)
        ).astype(BF16)
        edge = lon == LON_DEV - 1.0
        w01 = jnp.where(edge, w01, 0.0)
        w11 = jnp.where(edge, w11, 0.0)
        few = row[:EDGE_ROWS]
        hot_ref[LON_DEV : LON_DEV + EDGE_ROWS, at] = jnp.where(
            few == lat, w01, jnp.where(few == lat + 1.0, w11, 0.0)
        ).astype(BF16)
    hot_ref[LON_DEV + EDGE_ROWS :, :] = jnp.zeros((LANES - EDGE_ROWS, x_ref.shape[1]), BF16)
    sums = lax.dot_general(x_ref[...], hot_ref[...], NT, preferred_element_type=F32)
    north_ref[...] = sums[:, :LON_DEV].astype(BF16)
    block = east_ref.shape[0]
    east = sums[:block, LON_DEV:]
    for g in range(1, FOLD):
        east = east + pltpu.roll(sums[g * block : (g + 1) * block, LON_DEV:], g * PITCH, 1)
    east_ref[...] = east
    corner_ref[:block] = east
    corner_ref[block:] = east[:32]


def hot_rows(near_ref, far_ref, within, first, count):
    zero = jnp.zeros(near_ref.shape, BF16)
    hots = []
    for v in range(first, first + count):
        far_part = jnp.where(within == bf(v - 1), far_ref[...], zero) if v else zero
        hots.append(jnp.where(within == bf(v), near_ref[...], far_part))
    return jnp.concatenate(hots, axis=0)


def split_latitude(lat):
    group = jnp.floor(lat * (1.0 / SPAN))
    return group.astype(BF16), (lat - group * SPAN).astype(BF16)


def lower_kernel(x_ref, info_ref, acc_ref, near_ref, far_ref, left_ref, *, levels):
    rows, slots = x_ref.shape
    rest = levels % 8
    row = row_iota((LON_DEV, LANES)).astype(F32)
    for tile in range(slots // LANES):
        at = pl.ds(tile * LANES, LANES)
        w00, w01, w10, w11, _, lon = [info_ref[rest + i : rest + i + 1, at] for i in range(N_INFO)]
        here = row == lon
        after = row == lon + 1.0
        near_ref[:, at] = jnp.where(here, w00, jnp.where(after, w01, 0.0)).astype(BF16)
        far_ref[:, at] = jnp.where(here, w10, jnp.where(after, w11, 0.0)).astype(BF16)
    lat = info_ref[rest + 4 : rest + 5, :]
    group, within = split_latitude(lat)
    lat = lat.astype(BF16)
    x = x_ref[...]
    zero_x = jnp.zeros_like(x)
    for u in range(GROUPS):
        left_ref[u * rows : (u + 1) * rows, :] = jnp.where(group == bf(u), x, zero_x)
    zero = jnp.zeros((LON_DEV, slots), BF16)
    far = far_ref[...]
    hot = jnp.concatenate([jnp.where(lat == bf(SPAN * u - 1), far, zero) for u in range(1, GROUPS)], axis=0)
    seam = lax.dot_general(x, hot, NT, preferred_element_type=F32)
    for first in range(0, LOWER, 4):
        hot = hot_rows(near_ref, far_ref, within, first, 4)
        sums = lax.dot_general(left_ref[...], hot, NT, preferred_element_type=F32)
        for u in range(GROUPS):
            for i in range(4):
                value = sums[u * rows : (u + 1) * rows, i * LON_DEV : (i + 1) * LON_DEV]
                if first + i == 0 and u > 0:
                    value = value + seam[:, (u - 1) * LON_DEV : u * LON_DEV]
                acc_ref[u * LOWER + first + i] = value


def edge_column(fold, r, first_lane):
    parts = []
    for g in range(FOLD):
        shift = (LANES - g * PITCH - r) % LANES
        parts.append(pltpu.roll(fold, shift, 1) if shift else fold)
    return jnp.where(first_lane, jnp.concatenate(parts, axis=0), 0.0)


def upper_kernel(
    acc_ref, near_ref, far_ref, left_ref, info_ref, east_ref, out_hbm, south_ref, grid_ref, sems, *, levels
):
    rows = acc_ref.shape[1]
    rest = levels % 8
    first_lane = lane_iota((rows, LANES)) == 0
    copies = []

    def finish(r, value):
        value = value + edge_column(east_ref[...], r, first_lane)
        if r == 0:
            south_ref[...] = value
            return
        grid_ref[r] = value
        copy = pltpu.make_async_copy(grid_ref.at[r, 0:levels, :], out_hbm.at[:, r, :], sems.at[r])
        copy.start()
        copies.append(copy)

    for u in range(GROUPS):
        for v in range(LOWER):
            finish(u * SPAN + v, acc_ref[u * LOWER + v])
    _, within = split_latitude(info_ref[rest + 4 : rest + 5, :])
    for first in range(LOWER, SPAN, 2):
        hot = hot_rows(near_ref, far_ref, within, first, 2)
        sums = lax.dot_general(left_ref[...], hot, NT, preferred_element_type=F32)
        for u in range(GROUPS):
            for i in range(2):
                finish(
                    u * SPAN + first + i,
                    sums[u * rows : (u + 1) * rows, i * LON_DEV : (i + 1) * LON_DEV],
                )
    for copy in copies:
        copy.wait()


def last_kernel(south_ref, north_ref, corner_ref, grid_hbm, out_hbm, row_ref, sem):
    del grid_hbm
    first_lane = lane_iota(south_ref.shape) == 0
    passed = north_ref[...].astype(F32) + edge_column(corner_ref[: south_ref.shape[0] // FOLD], LAT_DEV, first_lane)
    row_ref[...] = south_ref[...] + jnp.where(lax.axis_index("band") > 0, passed, 0.0)
    copy = pltpu.make_async_copy(row_ref.at[0 : out_hbm.shape[0], :], out_hbm.at[:, 0, :], sem)
    copy.start()
    copy.wait()


def per_device(jacobian, departure, inv_var, frac, anchors, counts, *, n_band, n_lon):
    slots, levels = jacobian.shape
    devices = counts.shape[1]
    cap = slots // devices
    rows = -(-(levels + N_INFO) // 16) * 16
    half = rows // 2
    vmem = pl.BlockSpec(memory_space=pltpu.VMEM)
    hbm = pl.BlockSpec(memory_space=pltpu.HBM)
    params = pltpu.CompilerParams(vmem_limit_bytes=VMEM_LIMIT)
    struct = jax.ShapeDtypeStruct

    payload = pl.pallas_call(
        functools.partial(pack_kernel, cap=cap, lon_count=n_lon),
        out_shape=struct((devices, half, LANES), BF16),
        in_specs=[hbm] * 6,
        out_specs=hbm,
        scratch_shapes=[
            pltpu.VMEM((devices, half, LANES), BF16),
            pltpu.SMEM((1, devices), jnp.int32),
            pltpu.VMEM((levels, slots), BF16),
            pltpu.VMEM((1, slots), F32),
            pltpu.VMEM((1, slots), F32),
            pltpu.VMEM((2, slots), F32),
            pltpu.VMEM((2, slots), jnp.int32),
            pltpu.SemaphoreType.DMA((5 + JAC_CHUNKS + OUT_CHUNKS,)),
        ],
        compiler_params=pltpu.CompilerParams(vmem_limit_bytes=VMEM_ALL),
        name="pack",
    )(counts, jacobian.T, departure[None, :], inv_var[None, :], frac, anchors)

    received = lax.all_to_all(payload, ("band", "lon"), split_axis=0, concat_axis=0, tiled=True)

    tail_rows = rows - levels // 8 * 8
    x, info, east, north, corner = pl.pallas_call(
        functools.partial(rim_kernel, cap=cap, levels=levels),
        out_shape=(
            struct((rows, slots), BF16),
            struct((tail_rows, slots), F32),
            struct((rows // FOLD, LANES), F32),
            struct((rows, LANES), BF16),
            struct((rows // FOLD + 32, LANES), F32),
        ),
        in_specs=[vmem],
        out_specs=(vmem,) * 5,
        scratch_shapes=[pltpu.VMEM((2 * LANES, slots), BF16)],
        compiler_params=params,
        name="rim",
    )(received)

    bands, lons = range(n_band), range(n_lon)
    north_in = lax.ppermute(north, "band", [(i, (i + 1) % n_band) for i in bands])
    corner_in = lax.ppermute(
        corner,
        ("band", "lon"),
        [
            (i * n_lon + j, (i + 1) % n_band * n_lon + (j + (i + 1 < n_band)) % n_lon)
            for i in bands
            for j in lons
        ],
    )
    east_in = lax.ppermute(east, "lon", [(j, (j + 1) % n_lon) for j in lons])

    acc, near, far, left = pl.pallas_call(
        functools.partial(lower_kernel, levels=levels),
        out_shape=(
            struct((GROUPS * LOWER, rows, LANES), F32),
            struct((LON_DEV, slots), BF16),
            struct((LON_DEV, slots), BF16),
            struct((GROUPS * rows, slots), BF16),
        ),
        in_specs=[vmem] * 2,
        out_specs=(vmem,) * 4,
        compiler_params=params,
        name="lower",
    )(x, info)

    grid, south = pl.pallas_call(
        functools.partial(upper_kernel, levels=levels),
        out_shape=(struct((levels, LAT_DEV, LON_DEV), F32), struct((rows, LANES), F32)),
        in_specs=[vmem] * 6,
        out_specs=(hbm, vmem),
        scratch_shapes=[pltpu.VMEM((LAT_DEV, rows, LANES), F32), pltpu.SemaphoreType.DMA((LAT_DEV,))],
        compiler_params=params,
        name="upper",
    )(acc, near, far, left, info, east_in)

    return pl.pallas_call(
        last_kernel,
        out_shape=struct((levels, LAT_DEV, LON_DEV), F32),
        in_specs=[vmem, vmem, vmem, hbm],
        out_specs=hbm,
        scratch_shapes=[pltpu.VMEM((rows, LANES), F32), pltpu.SemaphoreType.DMA],
        input_output_aliases={3: 0},
        compiler_params=params,
        name="last",
    )(south, north_in, corner_in, grid)


def solution(mesh):
    both = ("band", "lon")
    return jax.shard_map(
        functools.partial(per_device, n_band=mesh.shape["band"], n_lon=mesh.shape["lon"]),
        mesh=mesh,
        in_specs=(P(both, None), P(both), P(both), P(None, both), P(None, both), P(both, None)),
        out_specs=P(None, "band", "lon"),
        check_vma=False,
    )
```
